256 devices in a mesh: seq: 8 (over x, core), mp: 32 (over y, z).
Axes of the slice: x: 4, y: 4, z: 8, core: 2. Of those that a mesh axis runs over, the one named last changes fastest.
Arguments:
- inputs: bfloat16 [1024, 12288], P('seq'), may hold values from -6 to 6
- out_grads: bfloat16 [1024, 12288], P('seq'), may hold values from -6 to 6
- w1_blocks: bfloat16 [192, 32, 128, 128], P('mp', 'seq'), may hold values from -0.109375 to 0.109375
- w1_rows: int32 [192, 32], P('mp', 'seq'), may hold values from 0 to 95, as said below
- w1_count: int32 [192], P('mp'), may hold values from 16 to 32, as said below
- w2_blocks: bfloat16 [192, 32, 128, 128], P('mp', 'seq'), may hold values from -0.109375 to 0.109375
- w2_cols: int32 [192, 32], P('mp', 'seq'), may hold values from 0 to 95, as said below
- w2_count: int32 [192], P('mp'), may hold values from 16 to 32, as said below
Outputs:
- input_grads: bfloat16 [1024, 12288], P('seq', 'mp')
- w1_grads: bfloat16 [192, 32, 128, 128], P('mp', 'seq')
- w2_grads: bfloat16 [192, 32, 128, 128], P('mp', 'seq')
The draws below stay inside these ranges and needn't reach their ends.
Inputs may be any that keep to these rules, and one draw needn't show every extreme that they name: `w1_rows`: in each hidden block column the 32 entries name distinct block rows; only the first w1_count entries are live. `w1_count`: some hidden block column holds 32 live blocks and some 32 // 2. `w2_cols`: in each hidden block row the 32 entries name distinct block columns; only the first w2_count entries are live. `w2_count`: some hidden block row holds 32 live blocks and some 32 // 2.
All inputs are finite; a program needn't handle non-finite values.
Results may differ from the reference program's by a relative error of at most 0.005.
Values may be sent and summed in bfloat16 or wider, within the bound.
A program may use at most 192 MiB of HBM per device.

```python
import jax
import jax.numpy as jnp
from jax import lax

D = 12288
BLOCK = 128
CAP = 32
TOKENS = 1024
NFB = 192
KB = 96


def slot_lists(key):
    panel_keys = jax.random.split(key, NFB)

    def one_panel(panel_key):
        return jax.random.permutation(panel_key, KB)[:CAP]
    return jax.vmap(one_panel)(panel_keys).astype(jnp.int32)


def stored_counts(key):
    first_key, second_key, third_key = jax.random.split(key, 3)
    counts = jax.random.randint(first_key, (NFB,), CAP // 2, CAP + 1)
    full_at = jax.random.randint(second_key, (), 0, NFB)
    low_at = (full_at + jax.random.randint(third_key, (), 1, NFB)) % NFB
    panel_ids = jnp.arange(NFB)
    counts = jnp.where(panel_ids == full_at, CAP, counts)
    counts = jnp.where(panel_ids == low_at, CAP // 2, counts)
    return counts.astype(jnp.int32)


def draw_w1_rows(key, part):
    key = jax.random.fold_in(key, 1)
    return slot_lists(key)


def draw_w1_count(key, part):
    key = jax.random.fold_in(key, 2)
    return stored_counts(key)


def draw_w2_cols(key, part):
    key = jax.random.fold_in(key, 3)
    return slot_lists(key)


def draw_w2_count(key, part):
    key = jax.random.fold_in(key, 4)
    return stored_counts(key)


def levels(key, shape, cuts, least, top_value):
    factor_of = 1.0
    for axis_at, shards_of in cuts:
        draws = jax.random.uniform(jax.random.fold_in(jax.random.fold_in(key, 6), axis_at), (shards_of,), jnp.float32, least / len(cuts), top_value / len(cuts))
        factor_of = factor_of * jnp.repeat(jnp.exp(draws), shape[axis_at] // shards_of).reshape((-1,) + (1,) * (len(shape) - 1 - axis_at))
    return factor_of


def bell_draw(stream_key, dims, deviation, limit, shards=(), held_as=jnp.bfloat16):
    factor_of = levels(stream_key, dims, shards, -0.22, 0.18) if shards else 1.0
    entries = jax.random.normal(stream_key, dims, jnp.float32) * deviation * factor_of
    return jnp.minimum(jnp.maximum(entries, -limit), limit).astype(held_as)


def setup_inputs(seed: int = 0) -> dict:
    streams_of = jax.random.split(jax.random.key(seed), 9)
    inputs = bell_draw(streams_of[0], (TOKENS, D), 1.0, 6.0, ((0, 8),))
    out_grads = bell_draw(streams_of[1], (TOKENS, D), 1.0, 6.0, ((0, 8),))
    w1_blocks = bell_draw(streams_of[2], (NFB, CAP, BLOCK, BLOCK), (CAP * BLOCK * 3 // 4) ** -0.5, 0.109375, ((0, 32), (1, 8)))
    w1_rows = draw_w1_rows(jax.random.fold_in(streams_of[8], 71), 0)
    w1_count = draw_w1_count(jax.random.fold_in(streams_of[8], 71), 0)
    w2_blocks = bell_draw(streams_of[5], (NFB, CAP, BLOCK, BLOCK), (CAP * BLOCK * 3 // 4) ** -0.5, 0.109375, ((0, 32), (1, 8)))
    w2_cols = draw_w2_cols(jax.random.fold_in(streams_of[8], 71), 0)
    w2_count = draw_w2_count(jax.random.fold_in(streams_of[8], 71), 0)
    return dict(inputs=inputs, out_grads=out_grads, w1_blocks=w1_blocks, w1_rows=w1_rows, w1_count=w1_count, w2_blocks=w2_blocks, w2_cols=w2_cols, w2_count=w2_count)


GELU_C = 0.7978845608028654
CUBIC = 0.044715


def gelu_value(values):
    tanh_arg = GELU_C * (values + CUBIC * values * values * values)
    return 0.5 * values * (1.0 + jnp.tanh(tanh_arg))


def gelu_slope(values):
    tanh_arg = GELU_C * (values + CUBIC * values * values * values)
    tanh_val = jnp.tanh(tanh_arg)
    return 0.5 * (1.0 + tanh_val) + 0.5 * values * (1.0 - tanh_val * tanh_val) * GELU_C * (1.0 + 3.0 * CUBIC * values * values)


def reference(inputs, out_grads, w1_blocks, w1_rows, w1_count, w2_blocks, w2_cols, w2_count):
    in_blocks = inputs.reshape(TOKENS, KB, BLOCK)
    grad_blocks = out_grads.reshape(TOKENS, KB, BLOCK)
    slot_ids = jnp.arange(CAP, dtype=jnp.int32)

    def panel(input_total, panel_data):
        w1_panel, row_ids, count_one, w2_panel, col_ids, count_two = panel_data
        live_one = (slot_ids < count_one).astype(jnp.float32)
        live_two = (slot_ids < count_two).astype(jnp.float32)
        w1_live = w1_panel.astype(jnp.float32) * live_one[:, None, None]
        w2_live = w2_panel.astype(jnp.float32) * live_two[:, None, None]
        in_picked = in_blocks[:, row_ids].astype(jnp.float32)
        grad_picked = grad_blocks[:, col_ids].astype(jnp.float32)
        hidden = jnp.einsum("tki,kij->tj", in_picked, w1_live)
        activation = gelu_value(hidden).astype(jnp.bfloat16)
        act_grad = jnp.einsum("tke,kje->tj", grad_picked, w2_live)
        grad_hidden = (act_grad * gelu_slope(hidden)).astype(jnp.bfloat16)
        grad_wide = grad_hidden.astype(jnp.float32)
        w1_part = (jnp.einsum("tki,tj->kij", in_picked, grad_wide) * live_one[:, None, None]).astype(jnp.bfloat16)
        w2_part = (jnp.einsum("tj,tke->kje", activation.astype(jnp.float32), grad_picked) * live_two[:, None, None]).astype(jnp.bfloat16)
        contrib = jnp.einsum("tj,kij->tki", grad_wide, w1_live)
        input_total = input_total.at[:, row_ids].add(contrib)
        return input_total, (w1_part, w2_part)

    start_total = jnp.zeros((TOKENS, KB, BLOCK), jnp.float32)
    input_total, (w1_grads, w2_grads) = lax.scan(panel, start_total, (w1_blocks, w1_rows, w1_count, w2_blocks, w2_cols, w2_count))
    return input_total.reshape(TOKENS, D).astype(jnp.bfloat16), w1_grads, w2_grads
```

```python
import jax
import jax.numpy as jnp
from jax import lax
from jax.experimental import pallas as pl
from jax.experimental.pallas import tpu as pltpu
from jax.sharding import PartitionSpec as P

GELU_C = 0.7978845608028654
CUBIC = 0.044715
BF16 = jnp.bfloat16
F32 = jnp.float32
MESH = pl.DeviceIdType.MESH
NT = (((1,), (1,)), ((), ()))

NX = 4
NY = 4
NZ = 8
COLS = 3
D_ORDER = (2, 1, 3, 0)


def gelu_both(h):
    arg = GELU_C * (h + CUBIC * h * h * h)
    t = jnp.tanh(arg)
    value = 0.5 * h * (1.0 + t)
    slope = 0.5 * (1.0 + t) + 0.5 * h * (1.0 - t * t) * GELU_C * (1.0 + 3.0 * CUBIC * h * h)
    return value, slope


def kernel(
    x_hbm, dy_hbm, w1_hbm, w2_hbm, pkt_hbm,
    dx_out, g1_out, g2_out,
    stx, sty, xf, dyf, w1a, w1b, w1c, w2a, w2b, w2c,
    idxv, invv, idx_sm, inv_sm,
    ghcat, ght, actt,
    d1a, d1b, d1c, d2a, d2b, d2c,
    r1, r2, rl1, rl2, rr1, rr2, rp1, rp2,
    dxo, pxs, prx, yrc, zs, zown, zrc,
    loc_sem, pk_s, pk_r, xs_s, xs_r, wd_s, wd_r, wp_s, wp_r, wf_s, wf_r,
    s1_s, s1_r, s2_s, s2_r, sp_s, sp_r, px_s, px_r, y_s, y_r, z_s, z_r,
):
    w1 = (w1a, w1b, w1c)
    w2 = (w2a, w2b, w2c)
    d1 = (d1a, d1b, d1c)
    d2 = (d2a, d2b, d2c)
    s = lax.axis_index("seq")
    m = lax.axis_index("mp")
    x = s // 2
    c = s % 2
    o = 1 - c
    xl = (x + 3) % 4
    xr = (x + 1) % 4
    xo = (x + 2) % 4
    y = m // NZ
    z = m % NZ
    pending = []

    def send(src, dst, ssem, rsem, dev):
        cp = pltpu.make_async_remote_copy(
            src_ref=src, dst_ref=dst, send_sem=ssem, recv_sem=rsem,
            device_id=dev, device_id_type=MESH,
        )
        cp.start()
        pending.append(cp)

    def arrived(ref, ssem, rsem):
        pltpu.make_async_remote_copy(
            src_ref=ref, dst_ref=ref, send_sem=ssem, recv_sem=rsem,
            device_id=(s, m), device_id_type=MESH,
        ).wait_recv()

    local = [
        pltpu.make_async_copy(x_hbm, stx, loc_sem.at[0]),
        pltpu.make_async_copy(dy_hbm, sty, loc_sem.at[1]),
        pltpu.make_async_copy(pkt_hbm, idxv.at[s], loc_sem.at[2]),
    ]
    wlocal = []
    for j in range(COLS):
        wlocal.append(
            (
                pltpu.make_async_copy(
                    w1_hbm.at[3 * c + j], w1[j].at[pl.ds(4 * s, 4)], loc_sem.at[3 + 2 * j]),
                pltpu.make_async_copy(
                    w2_hbm.at[3 * c + j], w2[j].at[pl.ds(4 * s, 4)], loc_sem.at[4 + 2 * j]),
            )
        )
    for cp in local:
        cp.start()
    for pair in wlocal:
        for cp in pair:
            cp.start()

    barrier = pltpu.get_barrier_semaphore()
    for e in range(1, 8):
        pl.semaphore_signal(barrier, inc=1, device_id=((s + e) % 8, m), device_id_type=MESH)
    for e in range(1, NY):
        pl.semaphore_signal(
            barrier, inc=1, device_id=(s, ((y + e) % NY) * NZ + z), device_id_type=MESH)
    for e in range(1, NZ):
        pl.semaphore_signal(
            barrier, inc=1, device_id=(s, y * NZ + (z + e) % NZ), device_id_type=MESH)
    pl.semaphore_wait(barrier, 7 + NY - 1 + NZ - 1)

    for e in range(1, 8):
        send(pkt_hbm, idxv.at[s], pk_s.at[e - 1], pk_r.at[e - 1], ((s + e) % 8, m))

    def direct(j):
        for w, (src, dst) in enumerate(((w1_hbm, w1[j]), (w2_hbm, w2[j]))):
            for way, xd in ((0, xr), (1, xl)):
                for cd in range(2):
                    send(
                        src.at[3 * cd + j], dst.at[pl.ds(4 * s, 4)],
                        wd_s.at[j, w, way, cd], wd_r.at[j, w, way, c], (xd * 2 + cd, m),
                    )
            send(
                src.at[3 * o + j], dst.at[pl.ds(4 * s, 4)],
                wp_s.at[j, w], wp_r.at[j, w], (x * 2 + o, m),
            )

    def from_neighbour(j, w, way):
        dst = (w1, w2)[w][j]
        xs = (xl, xr)[way]
        for cs in range(2):
            arrived(dst.at[pl.ds(8 * xs + 4 * cs, 4)], wd_s.at[j, w, way, cs], wd_r.at[j, w, way, cs])

    def forward(j):
        from_neighbour(j, 0, 0)
        send(w1[j].at[pl.ds(8 * xl, 8)], w1[j].at[pl.ds(8 * xl, 8)],
             wf_s.at[j, 0], wf_r.at[j, 0], (xr * 2 + c, m))
        from_neighbour(j, 1, 1)
        send(w2[j].at[pl.ds(8 * xr, 8)], w2[j].at[pl.ds(8 * xr, 8)],
             wf_s.at[j, 1], wf_r.at[j, 1], (xl * 2 + c, m))

    def complete(j):
        for cp in wlocal[j]:
            cp.wait()
        for w in range(2):
            arrived((w1, w2)[w][j].at[pl.ds(8 * x + 4 * o, 4)], wp_s.at[j, w], wp_r.at[j, w])
        from_neighbour(j, 0, 1)
        from_neighbour(j, 1, 0)
        for w in range(2):
            arrived((w1, w2)[w][j].at[pl.ds(8 * xo, 8)], wf_s.at[j, w], wf_r.at[j, w])

    direct(0)
    for at, (flat, full) in enumerate(((stx, xf), (sty, dyf))):
        local[at].wait()

        def regroup(r, carry):
            full[r, 0:128] = flat[:, pl.ds(pl.multiple_of(r * 128, 128), 128)]
            return carry

        lax.fori_loop(0, 96, regroup, 0)
        send(full.at[:, pl.ds(0, 128)], full.at[:, pl.ds(128, 128)],
             xs_s.at[at], xs_r.at[at], (x * 2 + o, m))
    direct(1)

    for j in range(COLS):
        w1[j][32] = jnp.zeros((128, 128), BF16)

    local[2].wait()
    for e in range(1, 8):
        arrived(idxv.at[(s + 8 - e) % 8], pk_s.at[e - 1], pk_r.at[e - 1])
    total = idxv[0, 8:16]
    for t in range(1, 8):
        total = total + idxv[t, 8:16]
    invv[...] = jnp.where(total > 0, total - 1, 32)
    to_sm = pltpu.make_async_copy(idxv, idx_sm, loc_sem.at[9])
    to_sm2 = pltpu.make_async_copy(invv, inv_sm, loc_sem.at[10])
    to_sm.start()
    to_sm2.start()
    to_sm.wait()
    to_sm2.wait()

    def picked(ref, who, col, first):
        return jnp.concatenate([ref[idx_sm[who, col, first + u]] for u in range(4)], axis=1)

    def forward_pass(j):
        col = 3 * c + j

        def body(p, carry):
            h, a = carry
            xs = picked(xf, p, col, 0)
            ws = w1[j][pl.ds(4 * p, 4)].reshape(512, 128)
            h = h + jnp.dot(xs, ws, preferred_element_type=F32)
            ys = picked(dyf, p, col, 4)
            vs = jnp.concatenate([w2[j][4 * p + u] for u in range(4)], axis=1)
            a = a + lax.dot_general(ys, vs, NT, preferred_element_type=F32)
            return h, a

        zero = jnp.zeros((256, 128), F32)
        h, a = lax.fori_loop(0, 8, body, (zero, zero))
        value, slope = gelu_both(h)
        grad = a * slope
        ghcat[:, j * 128:(j + 1) * 128] = grad.astype(BF16)
        ght[j] = grad.T.astype(BF16)
        actt[j] = value.T.astype(BF16)

    def weight_grads(j):
        col = 3 * c + j

        def body(q, carry):
            who = (2 * xo + q) % 8
            t1 = jnp.dot(ght[j], picked(xf, who, col, 0), preferred_element_type=F32)
            t2 = jnp.dot(actt[j], picked(dyf, who, col, 4), preferred_element_type=F32)
            for u in range(4):
                d1[j][4 * who + u] = t1[:, 128 * u:128 * (u + 1)].astype(BF16)
                d2[j][4 * who + u] = t2[:, 128 * u:128 * (u + 1)].astype(BF16)
            return carry

        lax.fori_loop(0, 8, body, 0)

    def stage_one(j):
        send(d1[j].at[pl.ds(8 * xo, 8)], r1.at[j], s1_s.at[j, 0], s1_r.at[j, 0], (xr * 2 + c, m))
        send(d2[j].at[pl.ds(8 * xo, 8)], r2.at[j], s1_s.at[j, 1], s1_r.at[j, 1], (xl * 2 + c, m))

    def stage_two_plain(j):
        col = 3 * c + j
        for co in range(2):
            send(d2[j].at[pl.ds(8 * xr + 4 * co, 4)], rl2.at[col],
                 s2_s.at[j, 1, 0, co], s2_r.at[1, 0, col], (xr * 2 + co, m))
            send(d1[j].at[pl.ds(8 * xl + 4 * co, 4)], rr1.at[col],
                 s2_s.at[j, 0, 1, co], s2_r.at[0, 1, col], (xl * 2 + co, m))
        send(d1[j].at[pl.ds(8 * x + 4 * o, 4)], rp1.at[j], sp_s.at[j, 0], sp_r.at[j, 0], (x * 2 + o, m))
        send(d2[j].at[pl.ds(8 * x + 4 * o, 4)], rp2.at[j], sp_s.at[j, 1], sp_r.at[j, 1], (x * 2 + o, m))

    def stage_two_added(j):
        col = 3 * c + j
        arrived(r1.at[j], s1_s.at[j, 0], s1_r.at[j, 0])

        def add1(k, carry):
            at = 8 * xr + k
            d1[j][at] = (d1[j][at].astype(F32) + r1[j, k].astype(F32)).astype(BF16)
            return carry

        lax.fori_loop(0, 8, add1, 0)
        for co in range(2):
            send(d1[j].at[pl.ds(8 * xr + 4 * co, 4)], rl1.at[col],
                 s2_s.at[j, 0, 0, co], s2_r.at[0, 0, col], (xr * 2 + co, m))
        arrived(r2.at[j], s1_s.at[j, 1], s1_r.at[j, 1])

        def add2(k, carry):
            at = 8 * xl + k
            d2[j][at] = (d2[j][at].astype(F32) + r2[j, k].astype(F32)).astype(BF16)
            return carry

        lax.fori_loop(0, 8, add2, 0)
        for co in range(2):
            send(d2[j].at[pl.ds(8 * xl + 4 * co, 4)], rr2.at[col],
                 s2_s.at[j, 1, 1, co], s2_r.at[1, 1, col], (xl * 2 + co, m))

    def finish(j):
        for cc, own in ((c, True), (o, False)):
            col = 3 * cc + j
            arrived(rr1.at[col], s2_s.at[j, 0, 1, 0], s2_r.at[0, 1, col])
            arrived(rl2.at[col], s2_s.at[j, 1, 0, 0], s2_r.at[1, 0, col])
            arrived(rl1.at[col], s2_s.at[j, 0, 0, 0], s2_r.at[0, 0, col])
            arrived(rr2.at[col], s2_s.at[j, 1, 1, 0], s2_r.at[1, 1, col])
            if not own:
                arrived(rp1.at[j], sp_s.at[j, 0], sp_r.at[j, 0])
                arrived(rp2.at[j], sp_s.at[j, 1], sp_r.at[j, 1])

            def body(k, carry):
                mine1 = d1[j][4 * s + k] if own else rp1[j, k]
                mine2 = d2[j][4 * s + k] if own else rp2[j, k]
                t1 = mine1.astype(F32) + rl1[col, k].astype(F32) + rr1[col, k].astype(F32)
                t2 = mine2.astype(F32) + rl2[col, k].astype(F32) + rr2[col, k].astype(F32)
                g1_out[col, k] = t1.T.astype(BF16)
                g2_out[col, k] = t2.astype(BF16)
                return carry

            lax.fori_loop(0, 4, body, 0)

    def input_chunk(d):
        yy = (y + d) % NY

        def body(q, carry):
            zz = (z + q + 1) % NZ
            base = (yy * NZ + zz) * 3
            rows = []
            for t in range(3):
                rows.append(
                    jnp.concatenate(
                        [w1[j][inv_sm[3 * c + j, base + t]] for j in range(COLS)], axis=1))
            rhs = jnp.concatenate(rows, axis=0)
            out = lax.dot_general(ghcat[...], rhs, NT, preferred_element_type=F32)
            dxo[d, q] = out[:128]
            pxs[d, q] = out[128:].astype(BF16)
            return carry

        lax.fori_loop(0, NZ, body, 0)
        send(pxs.at[d], prx.at[d], px_s.at[d], px_r.at[d], (x * 2 + o, m))

    def input_pair(d):
        arrived(prx.at[d], px_s.at[d], px_r.at[d])

        def body(q, carry):
            both = dxo[d, q] + prx[d, q].astype(F32)
            if d:
                prx[d, q] = both.astype(BF16)
            else:
                dxo[d, q] = both
            return carry

        if d:
            for half in range(2):
                lax.fori_loop(4 * half, 4 * half + 4, body, 0)
                send(prx.at[d, pl.ds(4 * half, 4)], yrc.at[d - 1, pl.ds(4 * half, 4)],
                     y_s.at[d - 1, half], y_r.at[d - 1, half], (s, ((y + d) % NY) * NZ + z))
        else:
            lax.fori_loop(0, NZ, body, 0)

    def input_sum(half):
        for d in range(1, NY):
            arrived(yrc.at[d - 1, pl.ds(4 * half, 4)], y_s.at[d - 1, half], y_r.at[d - 1, half])
        for q in range(4 * half, 4 * half + 4):
            both = dxo[0, q]
            for d in range(1, NY):
                both = both + yrc[d - 1, q].astype(F32)
            if q < NZ - 1:
                zs[q] = both.astype(BF16)
                send(zs.at[q], zrc.at[q], z_s.at[q], z_r.at[q], (s, y * NZ + (z + q + 1) % NZ))
            else:
                zown[...] = both

    forward(0)
    direct(2)
    forward(1)
    arrived(xf.at[:, pl.ds(128, 128)], xs_s.at[0], xs_r.at[0])
    arrived(dyf.at[:, pl.ds(128, 128)], xs_s.at[1], xs_r.at[1])
    complete(0)
    forward_pass(0)
    forward(2)
    complete(1)
    forward_pass(1)
    weight_grads(0)
    weight_grads(1)
    complete(2)
    stage_one(0)
    stage_one(1)
    forward_pass(2)
    input_chunk(D_ORDER[0])
    input_chunk(D_ORDER[1])
    input_pair(D_ORDER[0])
    input_chunk(D_ORDER[2])
    input_pair(D_ORDER[1])
    input_chunk(D_ORDER[3])
    input_pair(D_ORDER[2])
    stage_two_plain(0)
    stage_two_plain(1)
    weight_grads(2)
    stage_one(2)
    stage_two_plain(2)
    input_pair(D_ORDER[3])
    stage_two_added(0)
    stage_two_added(1)
    stage_two_added(2)
    input_sum(0)
    input_sum(1)
    finish(0)
    finish(1)
    for q in range(NZ - 1):
        arrived(zrc.at[q], z_s.at[q], z_r.at[q])
    whole = zown[...]
    for q in range(NZ - 1):
        whole = whole + zrc[q].astype(F32)
    dx_out[...] = whole.astype(BF16)
    finish(2)
    for cp in pending:
        cp.wait_send()


def per_device(inputs, out_grads, w1_blocks, w1_rows, w1_count, w2_blocks, w2_cols, w2_count):
    s = lax.axis_index("seq")
    own_ids = s * 4 + jnp.arange(4, dtype=jnp.int32)
    live_one = (own_ids[None, :] < w1_count[:, None])[:, :, None, None]
    live_two = (own_ids[None, :] < w2_count[:, None])[:, :, None, None]
    nothing = jnp.zeros((), BF16)
    w1m = jnp.where(live_one, w1_blocks, nothing)
    w2m = jnp.where(live_two, w2_blocks, nothing)
    lanes = jnp.arange(128, dtype=jnp.int32)
    slot_of = jnp.sum(
        jnp.where(w1_rows[:, :, None] == lanes[None, None, :], own_ids[None, :, None] + 1, 0), axis=1)
    named = jnp.concatenate([w1_rows, w2_cols], axis=1)
    packet = jnp.concatenate(
        [jnp.pad(named, ((0, 2), (0, 120))), jnp.pad(slot_of, ((0, 2), (0, 0)))], axis=0)

    any_space = pl.BlockSpec(memory_space=pl.ANY)
    vmem = pl.BlockSpec(memory_space=pltpu.VMEM)
    dma = pltpu.SemaphoreType.DMA
    w_scratch = [pltpu.VMEM((33, 128, 128), BF16)] * 3 + [pltpu.VMEM((32, 128, 128), BF16)] * 3
    d_scratch = [pltpu.VMEM((32, 128, 128), BF16)] * 6
    dx, g1, g2 = pl.pallas_call(
        kernel,
        out_shape=(
            jax.ShapeDtypeStruct((128, 384), BF16),
            jax.ShapeDtypeStruct((6, 4, 128, 128), BF16),
            jax.ShapeDtypeStruct((6, 4, 128, 128), BF16),
        ),
        in_specs=[any_space] * 5,
        out_specs=(vmem, vmem, vmem),
        scratch_shapes=[
            pltpu.VMEM((128, 12288), BF16),
            pltpu.VMEM((128, 12288), BF16),
            pltpu.VMEM((96, 256, 128), BF16),
            pltpu.VMEM((96, 256, 128), BF16),
            *w_scratch,
            pltpu.VMEM((8, 16, 128), jnp.int32),
            pltpu.VMEM((8, 128), jnp.int32),
            pltpu.SMEM((8, 16, 128), jnp.int32),
            pltpu.SMEM((8, 128), jnp.int32),
            pltpu.VMEM((256, 384), BF16),
            pltpu.VMEM((3, 128, 256), BF16),
            pltpu.VMEM((3, 128, 256), BF16),
            *d_scratch,
            pltpu.VMEM((3, 8, 128, 128), BF16),
            pltpu.VMEM((3, 8, 128, 128), BF16),
            pltpu.VMEM((6, 4, 128, 128), BF16),
            pltpu.VMEM((6, 4, 128, 128), BF16),
            pltpu.VMEM((6, 4, 128, 128), BF16),
            pltpu.VMEM((6, 4, 128, 128), BF16),
            pltpu.VMEM((3, 4, 128, 128), BF16),
            pltpu.VMEM((3, 4, 128, 128), BF16),
            pltpu.VMEM((4, 8, 128, 384), F32),
            pltpu.VMEM((4, 8, 128, 384), BF16),
            pltpu.VMEM((4, 8, 128, 384), BF16),
            pltpu.VMEM((3, 8, 128, 384), BF16),
            pltpu.VMEM((7, 128, 384), BF16),
            pltpu.VMEM((128, 384), F32),
            pltpu.VMEM((7, 128, 384), BF16),
            dma((11,)),
            dma((7,)), dma((7,)),
            dma((2,)), dma((2,)),
            dma((3, 2, 2, 2)), dma((3, 2, 2, 2)),
            dma((3, 2)), dma((3, 2)),
            dma((3, 2)), dma((3, 2)),
            dma((3, 2)), dma((3, 2)),
            dma((3, 2, 2, 2)), dma((2, 2, 6)),
            dma((3, 2)), dma((3, 2)),
            dma((4,)), dma((4,)),
            dma((3, 2)), dma((3, 2)),
            dma((7,)), dma((7,)),
        ],
        compiler_params=pltpu.CompilerParams(
            collective_id=0, has_side_effects=True, vmem_limit_bytes=60 * 1024 * 1024),
    )(inputs, out_grads, w1m, w2m, packet)
    return (
        dx,
        jnp.where(live_one, g1, nothing),
        jnp.where(live_two, g2, nothing),
    )


def solution(mesh):
    in_specs = (
        P("seq", None),
        P("seq", None),
        P("mp", "seq", None, None),
        P("mp", "seq"),
        P("mp"),
        P("mp", "seq", None, None),
        P("mp", "seq"),
        P("mp"),
    )
    out_specs = (P("seq", "mp"), P("mp", "seq", None, None), P("mp", "seq", None, None))
    return jax.shard_map(
        per_device, mesh=mesh, in_specs=in_specs, out_specs=out_specs, check_vma=False
    )
```

```python
import jax
import jax.numpy as jnp
from jax import lax
from jax.experimental import pallas as pl
from jax.experimental.pallas import tpu as pltpu
from jax.sharding import PartitionSpec as P

GELU_C = 0.7978845608028654
CUBIC = 0.044715
BF16 = jnp.bfloat16
F32 = jnp.float32
MESH = pl.DeviceIdType.MESH
NT = (((1,), (1,)), ((), ()))

NX = 4
NY = 4
NZ = 8
COLS = 3
D_ORDER = (2, 1, 3, 0)
GROUPS = 4


def gelu_both(h):
    arg = GELU_C * (h + CUBIC * h * h * h)
    t = jnp.tanh(arg)
    value = 0.5 * h * (1.0 + t)
    slope = 0.5 * (1.0 + t) + 0.5 * h * (1.0 - t * t) * GELU_C * (1.0 + 3.0 * CUBIC * h * h)
    return value, slope


def kernel(
    x_hbm, dy_hbm, w1_hbm, w2_hbm, rows_sm, count1_sm, cols_sm, count2_sm,
    dx_out, g1_out, g2_out,
    stx, sty, xf, dyf, w1a, w1b, w1c, w2a, w2b, w2c,
    pktv, idxv, invv, idx_sm, inv_sm,
    ghcat, ght, actt,
    d1a, d1b, d1c, d2a, d2b, d2c,
    r1, r2, rl1, rl2, rr1, rr2, rp1, rp2,
    dxo, pxs, prx, y1b, yrc, zs, zown, zrc,
    hello, loc_sem, pk_s, pk_r, xs_s, xs_r, wd_s, wd_r, wp_s, wp_r, wf_s, wf_r,
    s1_s, s1_r, s2_s, s2_r, sp_s, sp_r, px_s, px_r, y1_s, y1_r, y_s, y_r, z_s, z_r,
):
    w1 = (w1a, w1b, w1c)
    w2 = (w2a, w2b, w2c)
    d1 = (d1a, d1b, d1c)
    d2 = (d2a, d2b, d2c)
    s = lax.axis_index("seq")
    m = lax.axis_index("mp")
    x = s // 2
    c = s % 2
    o = 1 - c
    xl = (x + 3) % 4
    xr = (x + 1) % 4
    xo = (x + 2) % 4
    y = m // NZ
    z = m % NZ
    pending = []

    def send(src, dst, ssem, rsem, dev):
        cp = pltpu.make_async_remote_copy(
            src_ref=src, dst_ref=dst, send_sem=ssem, recv_sem=rsem,
            device_id=dev, device_id_type=MESH,
        )
        cp.start()
        pending.append(cp)

    def arrived(ref, ssem, rsem):
        pltpu.make_async_remote_copy(
            src_ref=ref, dst_ref=ref, send_sem=ssem, recv_sem=rsem,
            device_id=(s, m), device_id_type=MESH,
        ).wait_recv()

    local = [
        pltpu.make_async_copy(x_hbm, stx, loc_sem.at[0]),
        pltpu.make_async_copy(dy_hbm, sty, loc_sem.at[1]),
    ]
    wlocal = []
    for j in range(COLS):
        wlocal.append(
            (
                pltpu.make_async_copy(
                    w1_hbm.at[3 * c + j], w1[j].at[pl.ds(4 * s, 4)], loc_sem.at[3 + 2 * j]),
                pltpu.make_async_copy(
                    w2_hbm.at[3 * c + j], w2[j].at[pl.ds(4 * s, 4)], loc_sem.at[4 + 2 * j]),
            )
        )
    for cp in local:
        cp.start()
    for pair in wlocal:
        for cp in pair:
            cp.start()

    def at_z(e):
        return (s, y * NZ + (z + e) % NZ)

    barrier = pltpu.get_barrier_semaphore()
    for e in range(1, 8):
        pl.semaphore_signal(barrier, inc=1, device_id=((s + e) % 8, m), device_id_type=MESH)
    for e in range(1, NY):
        pl.semaphore_signal(
            barrier, inc=1, device_id=(s, ((y + e) % NY) * NZ + z), device_id_type=MESH)
    for e in (1, NZ - 1):
        pl.semaphore_signal(barrier, inc=1, device_id=at_z(e), device_id_type=MESH)

    sub = lax.broadcasted_iota(jnp.int32, (8, 128), 0)
    lane = lax.broadcasted_iota(jnp.int32, (8, 128), 1)
    named = jnp.zeros((8, 128), jnp.int32)
    slot_of = jnp.zeros((8, 128), jnp.int32)
    for col in range(6):
        for k in range(4):
            slot = 4 * s + k
            row = jnp.where(slot < count1_sm[col], rows_sm[k, col], 96)
            other = jnp.where(slot < count2_sm[col], cols_sm[k, col], 96)
            named = jnp.where((sub == col) & (lane == k), row, named)
            named = jnp.where((sub == col) & (lane == 4 + k), other, named)
            slot_of = jnp.where((sub == col) & (lane == row), slot + 1, slot_of)
    pktv[0:8] = named
    pktv[8:16] = slot_of

    pl.semaphore_wait(barrier, 7 + NY - 1 + 2)

    for e in range(1, 8):
        send(pktv, idxv.at[s], pk_s.at[e - 1], pk_r.at[e - 1], ((s + e) % 8, m))
    idxv[s] = pktv[...]
    for e in (1, NZ - 1):
        pl.semaphore_signal(hello.at[0], inc=1, device_id=at_z(e), device_id_type=MESH)

    def direct(j):
        for w, (src, dst) in enumerate(((w1_hbm, w1[j]), (w2_hbm, w2[j]))):
            for way, xd in ((0, xr), (1, xl)):
                for cd in range(2):
                    send(
                        src.at[3 * cd + j], dst.at[pl.ds(4 * s, 4)],
                        wd_s.at[j, w, way, cd], wd_r.at[j, w, way, c], (xd * 2 + cd, m),
                    )
            send(
                src.at[3 * o + j], dst.at[pl.ds(4 * s, 4)],
                wp_s.at[j, w], wp_r.at[j, w], (x * 2 + o, m),
            )

    def from_neighbour(j, w, way):
        dst = (w1, w2)[w][j]
        xs = (xl, xr)[way]
        for cs in range(2):
            arrived(dst.at[pl.ds(8 * xs + 4 * cs, 4)], wd_s.at[j, w, way, cs], wd_r.at[j, w, way, cs])

    def forward(j):
        from_neighbour(j, 0, 0)
        send(w1[j].at[pl.ds(8 * xl, 8)], w1[j].at[pl.ds(8 * xl, 8)],
             wf_s.at[j, 0], wf_r.at[j, 0], (xr * 2 + c, m))
        from_neighbour(j, 1, 1)
        send(w2[j].at[pl.ds(8 * xr, 8)], w2[j].at[pl.ds(8 * xr, 8)],
             wf_s.at[j, 1], wf_r.at[j, 1], (xl * 2 + c, m))

    def complete(j):
        for cp in wlocal[j]:
            cp.wait()
        for w in range(2):
            arrived((w1, w2)[w][j].at[pl.ds(8 * x + 4 * o, 4)], wp_s.at[j, w], wp_r.at[j, w])
        from_neighbour(j, 0, 1)
        from_neighbour(j, 1, 0)
        for w in range(2):
            arrived((w1, w2)[w][j].at[pl.ds(8 * xo, 8)], wf_s.at[j, w], wf_r.at[j, w])

    direct(0)
    direct(1)
    direct(2)

    for at, (flat, full) in enumerate(((stx, xf), (sty, dyf))):
        local[at].wait()

        def regroup(r, carry):
            full[r, 0:128] = flat[:, pl.ds(pl.multiple_of(r * 128, 128), 128)]
            return carry

        lax.fori_loop(0, 96, regroup, 0)
        send(full.at[pl.ds(0, 96), pl.ds(0, 128)], full.at[pl.ds(0, 96), pl.ds(128, 128)],
             xs_s.at[at], xs_r.at[at], (x * 2 + o, m))
        full[96] = jnp.zeros((256, 128), BF16)

    for j in range(COLS):
        w1[j][32] = jnp.zeros((128, 128), BF16)

    pl.semaphore_wait(hello.at[0], 2)
    for e in (2, NZ - 2):
        pl.semaphore_signal(hello.at[1], inc=1, device_id=at_z(e), device_id_type=MESH)

    for e in range(1, 8):
        arrived(idxv.at[(s + 8 - e) % 8], pk_s.at[e - 1], pk_r.at[e - 1])
    total = idxv[0, 8:16]
    for t in range(1, 8):
        total = total + idxv[t, 8:16]
    invv[...] = jnp.where(total > 0, total - 1, 32)
    to_sm = pltpu.make_async_copy(idxv, idx_sm, loc_sem.at[9])
    to_sm2 = pltpu.make_async_copy(invv, inv_sm, loc_sem.at[10])
    to_sm.start()
    to_sm2.start()
    to_sm.wait()
    to_sm2.wait()

    def picked(ref, who, col, first):
        return jnp.concatenate([ref[idx_sm[who, col, first + u]] for u in range(4)], axis=1)

    def forward_pass(j):
        col = 3 * c + j

        def body(p, carry):
            h, a = carry
            xs = picked(xf, p, col, 0)
            ws = w1[j][pl.ds(4 * p, 4)].reshape(512, 128)
            h = h + jnp.dot(xs, ws, preferred_element_type=F32)
            ys = picked(dyf, p, col, 4)
            vs = jnp.concatenate([w2[j][4 * p + u] for u in range(4)], axis=1)
            a = a + lax.dot_general(ys, vs, NT, preferred_element_type=F32)
            return h, a

        zero = jnp.zeros((256, 128), F32)
        h, a = lax.fori_loop(0, 8, body, (zero, zero))
        value, slope = gelu_both(h)
        grad = a * slope
        ghcat[:, j * 128:(j + 1) * 128] = grad.astype(BF16)
        ght[j] = grad.T.astype(BF16)
        actt[j] = value.T.astype(BF16)

    def weight_grads(j):
        col = 3 * c + j

        def body(q, carry):
            who = (2 * xo + q) % 8
            t1 = jnp.dot(ght[j], picked(xf, who, col, 0), preferred_element_type=F32)
            t2 = jnp.dot(actt[j], picked(dyf, who, col, 4), preferred_element_type=F32)
            for u in range(4):
                d1[j][4 * who + u] = t1[:, 128 * u:128 * (u + 1)].astype(BF16)
                d2[j][4 * who + u] = t2[:, 128 * u:128 * (u + 1)].astype(BF16)
            return carry

        lax.fori_loop(0, 8, body, 0)

    def stage_one(j):
        send(d1[j].at[pl.ds(8 * xo, 8)], r1.at[j], s1_s.at[j, 0], s1_r.at[j, 0], (xr * 2 + c, m))
        send(d2[j].at[pl.ds(8 * xo, 8)], r2.at[j], s1_s.at[j, 1], s1_r.at[j, 1], (xl * 2 + c, m))

    def stage_two_plain(j):
        col = 3 * c + j
        for co in range(2):
            send(d2[j].at[pl.ds(8 * xr + 4 * co, 4)], rl2.at[col],
                 s2_s.at[j, 1, 0, co], s2_r.at[1, 0, col], (xr * 2 + co, m))
            send(d1[j].at[pl.ds(8 * xl + 4 * co, 4)], rr1.at[col],
                 s2_s.at[j, 0, 1, co], s2_r.at[0, 1, col], (xl * 2 + co, m))
        send(d1[j].at[pl.ds(8 * x + 4 * o, 4)], rp1.at[j], sp_s.at[j, 0], sp_r.at[j, 0], (x * 2 + o, m))
        send(d2[j].at[pl.ds(8 * x + 4 * o, 4)], rp2.at[j], sp_s.at[j, 1], sp_r.at[j, 1], (x * 2 + o, m))

    def stage_two_added(j):
        col = 3 * c + j
        arrived(r1.at[j], s1_s.at[j, 0], s1_r.at[j, 0])

        def add1(k, carry):
            at = 8 * xr + k
            d1[j][at] = (d1[j][at].astype(F32) + r1[j, k].astype(F32)).astype(BF16)
            return carry

        lax.fori_loop(0, 8, add1, 0)
        for co in range(2):
            send(d1[j].at[pl.ds(8 * xr + 4 * co, 4)], rl1.at[col],
                 s2_s.at[j, 0, 0, co], s2_r.at[0, 0, col], (xr * 2 + co, m))
        arrived(r2.at[j], s1_s.at[j, 1], s1_r.at[j, 1])

        def add2(k, carry):
            at = 8 * xl + k
            d2[j][at] = (d2[j][at].astype(F32) + r2[j, k].astype(F32)).astype(BF16)
            return carry

        lax.fori_loop(0, 8, add2, 0)
        for co in range(2):
            send(d2[j].at[pl.ds(8 * xl + 4 * co, 4)], rr2.at[col],
                 s2_s.at[j, 1, 1, co], s2_r.at[1, 1, col], (xl * 2 + co, m))

    def finish(j):
        for cc, own in ((c, True), (o, False)):
            col = 3 * cc + j
            arrived(rr1.at[col], s2_s.at[j, 0, 1, 0], s2_r.at[0, 1, col])
            arrived(rl2.at[col], s2_s.at[j, 1, 0, 0], s2_r.at[1, 0, col])
            arrived(rl1.at[col], s2_s.at[j, 0, 0, 0], s2_r.at[0, 0, col])
            arrived(rr2.at[col], s2_s.at[j, 1, 1, 0], s2_r.at[1, 1, col])
            if not own:
                arrived(rp1.at[j], sp_s.at[j, 0], sp_r.at[j, 0])
                arrived(rp2.at[j], sp_s.at[j, 1], sp_r.at[j, 1])

            def body(k, carry):
                mine1 = d1[j][4 * s + k] if own else rp1[j, k]
                mine2 = d2[j][4 * s + k] if own else rp2[j, k]
                t1 = mine1.astype(F32) + rl1[col, k].astype(F32) + rr1[col, k].astype(F32)
                t2 = mine2.astype(F32) + rl2[col, k].astype(F32) + rr2[col, k].astype(F32)
                g1_out[col, k] = t1.T.astype(BF16)
                g2_out[col, k] = t2.astype(BF16)
                return carry

            lax.fori_loop(0, 4, body, 0)

    def group(ref, d, g):
        return ref.at[d, pl.ds(2 * g, 2)]

    def input_group(g):
        for d in D_ORDER:
            yy = (y + d) % NY

            def body(q, carry):
                zz = (z + q + 1) % NZ
                base = (yy * NZ + zz) * 3
                rows = []
                for t in range(3):
                    rows.append(
                        jnp.concatenate(
                            [w1[j][inv_sm[3 * c + j, base + t]] for j in range(COLS)], axis=1))
                rhs = jnp.concatenate(rows, axis=0)
                out = lax.dot_general(ghcat[...], rhs, NT, preferred_element_type=F32)
                dxo[d, q] = out[:128]
                pxs[d, q] = out[128:].astype(BF16)
                return carry

            lax.fori_loop(2 * g, 2 * g + 2, body, 0)
            send(group(pxs, d, g), group(prx, d, g), px_s.at[d, g], px_r.at[d, g], (x * 2 + o, m))

    def to_y(d, g):
        send(group(prx, d, g), yrc.at[d // 2, pl.ds(2 * g, 2)],
             y_s.at[d // 2, g], y_r.at[d // 2, g], (s, ((y + d) % NY) * NZ + z))

    def input_pair(g):
        step = 1 if g % 2 == 0 else 3
        for d in D_ORDER:
            arrived(group(prx, d, g), px_s.at[d, g], px_r.at[d, g])
            sent = d in (2, 4 - step)

            def body(q, carry):
                both = dxo[d, q] + prx[d, q].astype(F32)
                if sent:
                    prx[d, q] = both.astype(BF16)
                else:
                    dxo[d, q] = both
                return carry

            lax.fori_loop(2 * g, 2 * g + 2, body, 0)
            if d == 2:
                send(group(prx, 2, g), y1b.at[g], y1_s.at[g], y1_r.at[g],
                     (s, ((y + step) % NY) * NZ + z))
            elif sent:
                to_y(d, g)

    def input_added(g):
        d = 1 if g % 2 == 0 else 3
        arrived(y1b.at[g], y1_s.at[g], y1_r.at[g])
        for i in range(2):
            q = 2 * g + i
            prx[d, q] = (dxo[d, q] + y1b[g, i].astype(F32)).astype(BF16)
        to_y(d, g)

    def input_sum(g):
        for i in range(2):
            arrived(yrc.at[i, pl.ds(2 * g, 2)], y_s.at[i, g], y_r.at[i, g])
        for q in (2 * g, 2 * g + 1):
            both = dxo[0, q] + yrc[0, q].astype(F32) + yrc[1, q].astype(F32)
            if q < NZ - 1:
                zs[q] = both.astype(BF16)
                send(zs.at[q], zrc.at[q], z_s.at[q], z_r.at[q], at_z(q + 1))
            else:
                zown[...] = both

    def input_last():
        whole = zown[...]
        for q in range(NZ - 1):
            arrived(zrc.at[q], z_s.at[q], z_r.at[q])
            whole = whole + zrc[q].astype(F32)
        dx_out[...] = whole.astype(BF16)

    forward(0)
    forward(1)
    arrived(xf.at[pl.ds(0, 96), pl.ds(128, 128)], xs_s.at[0], xs_r.at[0])
    arrived(dyf.at[pl.ds(0, 96), pl.ds(128, 128)], xs_s.at[1], xs_r.at[1])
    pl.semaphore_wait(hello.at[1], 2)
    complete(0)
    forward_pass(0)
    forward(2)
    complete(1)
    forward_pass(1)
    weight_grads(0)
    weight_grads(1)
    complete(2)
    stage_one(0)
    stage_one(1)
    stage_two_plain(0)
    stage_two_plain(1)
    forward_pass(2)
    input_group(0)
    input_group(1)
    input_pair(0)
    input_group(2)
    input_pair(1)
    stage_two_added(0)
    input_group(3)
    input_added(0)
    input_pair(2)
    input_added(1)
    stage_two_added(1)
    input_pair(3)
    weight_grads(2)
    stage_one(2)
    stage_two_plain(2)
    input_sum(0)
    input_added(2)
    input_sum(1)
    input_added(3)
    stage_two_added(2)
    input_sum(2)
    input_sum(3)
    finish(0)
    finish(1)
    input_last()
    finish(2)
    for cp in pending:
        cp.wait_send()


def copy_out(dx, g1, g2, dx_out, g1_out, g2_out, sem):
    copies = [pltpu.make_async_copy(dx, dx_out, sem.at[12])]
    for col in range(6):
        copies.append(pltpu.make_async_copy(g1.at[col], g1_out.at[col], sem.at[2 * col]))
        copies.append(pltpu.make_async_copy(g2.at[col], g2_out.at[col], sem.at[2 * col + 1]))
    for cp in copies:
        cp.start()
    for cp in copies:
        cp.wait()


def per_device(inputs, out_grads, w1_blocks, w1_rows, w1_count, w2_blocks, w2_cols, w2_count):
    any_space = pl.BlockSpec(memory_space=pl.ANY)
    vmem = pl.BlockSpec(memory_space=pltpu.VMEM)
    smem = pl.BlockSpec(memory_space=pltpu.SMEM)
    dma = pltpu.SemaphoreType.DMA
    w_scratch = [pltpu.VMEM((33, 128, 128), BF16)] * 3 + [pltpu.VMEM((32, 128, 128), BF16)] * 3
    d_scratch = [pltpu.VMEM((32, 128, 128), BF16)] * 6
    shapes = (
        jax.ShapeDtypeStruct((128, 384), BF16),
        jax.ShapeDtypeStruct((6, 4, 128, 128), BF16),
        jax.ShapeDtypeStruct((6, 4, 128, 128), BF16),
    )
    grads = pl.pallas_call(
        kernel,
        out_shape=shapes,
        in_specs=[any_space] * 4 + [smem] * 4,
        out_specs=(vmem, vmem, vmem),
        scratch_shapes=[
            pltpu.VMEM((128, 12288), BF16),
            pltpu.VMEM((128, 12288), BF16),
            pltpu.VMEM((97, 256, 128), BF16),
            pltpu.VMEM((97, 256, 128), BF16),
            *w_scratch,
            pltpu.VMEM((16, 128), jnp.int32),
            pltpu.VMEM((8, 16, 128), jnp.int32),
            pltpu.VMEM((8, 128), jnp.int32),
            pltpu.SMEM((8, 16, 128), jnp.int32),
            pltpu.SMEM((8, 128), jnp.int32),
            pltpu.VMEM((256, 384), BF16),
            pltpu.VMEM((3, 128, 256), BF16),
            pltpu.VMEM((3, 128, 256), BF16),
            *d_scratch,
            pltpu.VMEM((3, 8, 128, 128), BF16),
            pltpu.VMEM((3, 8, 128, 128), BF16),
            pltpu.VMEM((6, 4, 128, 128), BF16),
            pltpu.VMEM((6, 4, 128, 128), BF16),
            pltpu.VMEM((6, 4, 128, 128), BF16),
            pltpu.VMEM((6, 4, 128, 128), BF16),
            pltpu.VMEM((3, 4, 128, 128), BF16),
            pltpu.VMEM((3, 4, 128, 128), BF16),
            pltpu.VMEM((4, 8, 128, 384), F32),
            pltpu.VMEM((4, 8, 128, 384), BF16),
            pltpu.VMEM((4, 8, 128, 384), BF16),
            pltpu.VMEM((4, 2, 128, 384), BF16),
            pltpu.VMEM((2, 8, 128, 384), BF16),
            pltpu.VMEM((7, 128, 384), BF16),
            pltpu.VMEM((128, 384), F32),
            pltpu.VMEM((7, 128, 384), BF16),
            pltpu.SemaphoreType.REGULAR((2,)),
            dma((11,)),
            dma((7,)), dma((7,)),
            dma((2,)), dma((2,)),
            dma((3, 2, 2, 2)), dma((3, 2, 2, 2)),
            dma((3, 2)), dma((3, 2)),
            dma((3, 2)), dma((3, 2)),
            dma((3, 2)), dma((3, 2)),
            dma((3, 2, 2, 2)), dma((2, 2, 6)),
            dma((3, 2)), dma((3, 2)),
            dma((4, 4)), dma((4, 4)),
            dma((4,)), dma((4,)),
            dma((2, 4)), dma((2, 4)),
            dma((7,)), dma((7,)),
        ],
        compiler_params=pltpu.CompilerParams(
            collective_id=0, has_side_effects=True, vmem_limit_bytes=60 * 1024 * 1024),
    )(inputs, out_grads, w1_blocks, w2_blocks, w1_rows.T, w1_count, w2_cols.T, w2_count)
    return pl.pallas_call(
        copy_out,
        out_shape=shapes,
        in_specs=[any_space] * 3,
        out_specs=(any_space,) * 3,
        scratch_shapes=[dma((13,))],
    )(*grads)


def solution(mesh):
    in_specs = (
        P("seq", None),
        P("seq", None),
        P("mp", "seq", None, None),
        P("mp", "seq"),
        P("mp"),
        P("mp", "seq", None, None),
        P("mp", "seq"),
        P("mp"),
    )
    out_specs = (P("seq", "mp"), P("mp", "seq", None, None), P("mp", "seq", None, None))
    return jax.shard_map(
        per_device, mesh=mesh, in_specs=in_specs, out_specs=out_specs, check_vma=False
    )
```

```python
import jax
import jax.numpy as jnp
from jax import lax
from jax.experimental import pallas as pl
from jax.experimental.pallas import tpu as pltpu
from jax.sharding import PartitionSpec as P

GELU_C = 0.7978845608028654
CUBIC = 0.044715
BF16 = jnp.bfloat16
F32 = jnp.float32
MESH = pl.DeviceIdType.MESH
NT = (((1,), (1,)), ((), ()))

NX = 4
NY = 4
NZ = 8
COLS = 3
D_ORDER = (2, 1, 3, 0)
GROUPS = 4


def gelu_both(h):
    arg = GELU_C * (h + CUBIC * h * h * h)
    t = jnp.tanh(arg)
    value = 0.5 * h * (1.0 + t)
    slope = 0.5 * (1.0 + t) + 0.5 * h * (1.0 - t * t) * GELU_C * (1.0 + 3.0 * CUBIC * h * h)
    return value, slope


def kernel(
    x_hbm, dy_hbm, w1_hbm, w2_hbm, rows_sm, count1_sm, cols_sm, count2_sm,
    dx_out, g1_out, g2_out,
    stx, sty, xf, dyf, w1a, w1b, w1c, w2a, w2b, w2c,
    pktv, idxv, invv, idx_sm, inv_sm,
    ghcat, ght, actt,
    d1a, d1b, d1c, d2a, d2b, d2c,
    r1, r2, rl1, rl2, rr1, rr2, rp1, rp2,
    dxo, pxs, prx, y1b, yrc, zs, zown, zrc,
    hello, loc_sem, pk_s, pk_r, xs_s, xs_r, wd_s, wd_r, wp_s, wp_r, wf_s, wf_r,
    s1_s, s1_r, s2_s, s2_r, sp_s, sp_r, px_s, px_r, y1_s, y1_r, y_s, y_r, z_s, z_r,
):
    w1 = (w1a, w1b, w1c)
    w2 = (w2a, w2b, w2c)
    d1 = (d1a, d1b, d1c)
    d2 = (d2a, d2b, d2c)
    s = lax.axis_index("seq")
    m = lax.axis_index("mp")
    x = s // 2
    c = s % 2
    o = 1 - c
    xl = (x + 3) % 4
    xr = (x + 1) % 4
    xo = (x + 2) % 4
    y = m // NZ
    z = m % NZ
    pending = []

    def send(src, dst, ssem, rsem, dev):
        cp = pltpu.make_async_remote_copy(
            src_ref=src, dst_ref=dst, send_sem=ssem, recv_sem=rsem,
            device_id=dev, device_id_type=MESH,
        )
        cp.start()
        pending.append(cp)

    def arrived(ref, ssem, rsem):
        pltpu.make_async_remote_copy(
            src_ref=ref, dst_ref=ref, send_sem=ssem, recv_sem=rsem,
            device_id=(s, m), device_id_type=MESH,
        ).wait_recv()

    local = [
        pltpu.make_async_copy(x_hbm, stx, loc_sem.at[0]),
        pltpu.make_async_copy(dy_hbm, sty, loc_sem.at[1]),
    ]
    wlocal = []
    for j in range(COLS):
        wlocal.append(
            (
                pltpu.make_async_copy(
                    w1_hbm.at[3 * c + j], w1[j].at[pl.ds(4 * s, 4)], loc_sem.at[3 + 2 * j]),
                pltpu.make_async_copy(
                    w2_hbm.at[3 * c + j], w2[j].at[pl.ds(4 * s, 4)], loc_sem.at[4 + 2 * j]),
            )
        )
    for cp in local:
        cp.start()
    for pair in wlocal:
        for cp in pair:
            cp.start()

    def at_z(e):
        return (s, y * NZ + (z + e) % NZ)

    barrier = pltpu.get_barrier_semaphore()
    for e in range(1, 8):
        pl.semaphore_signal(barrier, inc=1, device_id=((s + e) % 8, m), device_id_type=MESH)
    for e in range(1, NY):
        pl.semaphore_signal(
            barrier, inc=1, device_id=(s, ((y + e) % NY) * NZ + z), device_id_type=MESH)
    for e in (1, NZ - 1):
        pl.semaphore_signal(barrier, inc=1, device_id=at_z(e), device_id_type=MESH)

    sub = lax.broadcasted_iota(jnp.int32, (8, 128), 0)
    lane = lax.broadcasted_iota(jnp.int32, (8, 128), 1)
    named = jnp.zeros((8, 128), jnp.int32)
    slot_of = jnp.zeros((8, 128), jnp.int32)
    for col in range(6):
        for k in range(4):
            slot = 4 * s + k
            row = jnp.where(slot < count1_sm[col], rows_sm[k, col], 96)
            other = jnp.where(slot < count2_sm[col], cols_sm[k, col], 96)
            named = jnp.where((sub == col) & (lane == k), row, named)
            named = jnp.where((sub == col) & (lane == 4 + k), other, named)
            slot_of = jnp.where((sub == col) & (lane == row), slot + 1, slot_of)
    pktv[0:8] = named
    pktv[8:16] = slot_of

    pl.semaphore_wait(barrier, 7 + NY - 1 + 2)

    for e in range(1, 8):
        send(pktv, idxv.at[s], pk_s.at[e - 1], pk_r.at[e - 1], ((s + e) % 8, m))
    idxv[s] = pktv[...]
    for e in (1, NZ - 1):
        pl.semaphore_signal(hello.at[0], inc=1, device_id=at_z(e), device_id_type=MESH)

    def direct(j):
        for w, (src, dst) in enumerate(((w1_hbm, w1[j]), (w2_hbm, w2[j]))):
            for way, xd in ((0, xr), (1, xl)):
                for cd in range(2):
                    send(
                        src.at[3 * cd + j], dst.at[pl.ds(4 * s, 4)],
                        wd_s.at[j, w, way, cd], wd_r.at[j, w, way, c], (xd * 2 + cd, m),
                    )
            send(
                src.at[3 * o + j], dst.at[pl.ds(4 * s, 4)],
                wp_s.at[j, w], wp_r.at[j, w], (x * 2 + o, m),
            )

    def from_neighbour(j, w, way):
        dst = (w1, w2)[w][j]
        xs = (xl, xr)[way]
        for cs in range(2):
            arrived(dst.at[pl.ds(8 * xs + 4 * cs, 4)], wd_s.at[j, w, way, cs], wd_r.at[j, w, way, cs])

    def forward(j):
        from_neighbour(j, 0, 0)
        send(w1[j].at[pl.ds(8 * xl, 8)], w1[j].at[pl.ds(8 * xl, 8)],
             wf_s.at[j, 0], wf_r.at[j, 0], (xr * 2 + c, m))
        from_neighbour(j, 1, 1)
        send(w2[j].at[pl.ds(8 * xr, 8)], w2[j].at[pl.ds(8 * xr, 8)],
             wf_s.at[j, 1], wf_r.at[j, 1], (xl * 2 + c, m))

    def complete(j):
        for cp in wlocal[j]:
            cp.wait()
        for w in range(2):
            arrived((w1, w2)[w][j].at[pl.ds(8 * x + 4 * o, 4)], wp_s.at[j, w], wp_r.at[j, w])
        from_neighbour(j, 0, 1)
        from_neighbour(j, 1, 0)
        for w in range(2):
            arrived((w1, w2)[w][j].at[pl.ds(8 * xo, 8)], wf_s.at[j, w], wf_r.at[j, w])

    direct(0)
    direct(1)
    direct(2)

    for at, (flat, full) in enumerate(((stx, xf), (sty, dyf))):
        local[at].wait()

        def regroup(r, carry):
            full[r, 0:128] = flat[:, pl.ds(pl.multiple_of(r * 128, 128), 128)]
            return carry

        lax.fori_loop(0, 96, regroup, 0)
        send(full.at[pl.ds(0, 96), pl.ds(0, 128)], full.at[pl.ds(0, 96), pl.ds(128, 128)],
             xs_s.at[at], xs_r.at[at], (x * 2 + o, m))
        full[96] = jnp.zeros((256, 128), BF16)

    for j in range(COLS):
        w1[j][32] = jnp.zeros((128, 128), BF16)

    pl.semaphore_wait(hello.at[0], 2)
    for e in (2, NZ - 2):
        pl.semaphore_signal(hello.at[1], inc=1, device_id=at_z(e), device_id_type=MESH)

    for e in range(1, 8):
        arrived(idxv.at[(s + 8 - e) % 8], pk_s.at[e - 1], pk_r.at[e - 1])
    total = idxv[0, 8:16]
    for t in range(1, 8):
        total = total + idxv[t, 8:16]
    invv[...] = jnp.where(total > 0, total - 1, 32)
    to_sm = pltpu.make_async_copy(idxv, idx_sm, loc_sem.at[9])
    to_sm2 = pltpu.make_async_copy(invv, inv_sm, loc_sem.at[10])
    to_sm.start()
    to_sm2.start()
    to_sm.wait()
    to_sm2.wait()

    def picked(ref, who, col, first):
        return jnp.concatenate([ref[idx_sm[who, col, first + u]] for u in range(4)], axis=1)

    def forward_pass(j):
        col = 3 * c + j

        def body(p, carry):
            h, a = carry
            xs = picked(xf, p, col, 0)
            ws = w1[j][pl.ds(4 * p, 4)].reshape(512, 128)
            h = h + jnp.dot(xs, ws, preferred_element_type=F32)
            ys = picked(dyf, p, col, 4)
            vs = jnp.concatenate([w2[j][4 * p + u] for u in range(4)], axis=1)
            a = a + lax.dot_general(ys, vs, NT, preferred_element_type=F32)
            return h, a

        zero = jnp.zeros((256, 128), F32)
        h, a = lax.fori_loop(0, 8, body, (zero, zero))
        value, slope = gelu_both(h)
        grad = a * slope
        ghcat[:, j * 128:(j + 1) * 128] = grad.astype(BF16)
        ght[j] = grad.T.astype(BF16)
        actt[j] = value.T.astype(BF16)

    def weight_grads(j):
        col = 3 * c + j

        def body(q, carry):
            who = (2 * xo + q) % 8
            t1 = jnp.dot(ght[j], picked(xf, who, col, 0), preferred_element_type=F32)
            t2 = jnp.dot(actt[j], picked(dyf, who, col, 4), preferred_element_type=F32)
            for u in range(4):
                d1[j][4 * who + u] = t1[:, 128 * u:128 * (u + 1)].astype(BF16)
                d2[j][4 * who + u] = t2[:, 128 * u:128 * (u + 1)].astype(BF16)
            return carry

        lax.fori_loop(0, 8, body, 0)

    def stage_one(j):
        send(d1[j].at[pl.ds(8 * xo, 8)], r1.at[j], s1_s.at[j, 0], s1_r.at[j, 0], (xr * 2 + c, m))
        send(d2[j].at[pl.ds(8 * xo, 8)], r2.at[j], s1_s.at[j, 1], s1_r.at[j, 1], (xl * 2 + c, m))

    def stage_two_plain(j):
        col = 3 * c + j
        for co in range(2):
            send(d2[j].at[pl.ds(8 * xr + 4 * co, 4)], rl2.at[col],
                 s2_s.at[j, 1, 0, co], s2_r.at[1, 0, col], (xr * 2 + co, m))
            send(d1[j].at[pl.ds(8 * xl + 4 * co, 4)], rr1.at[col],
                 s2_s.at[j, 0, 1, co], s2_r.at[0, 1, col], (xl * 2 + co, m))
        send(d1[j].at[pl.ds(8 * x + 4 * o, 4)], rp1.at[j], sp_s.at[j, 0], sp_r.at[j, 0], (x * 2 + o, m))
        send(d2[j].at[pl.ds(8 * x + 4 * o, 4)], rp2.at[j], sp_s.at[j, 1], sp_r.at[j, 1], (x * 2 + o, m))

    def stage_two_added(j):
        col = 3 * c + j
        arrived(r1.at[j], s1_s.at[j, 0], s1_r.at[j, 0])

        def add1(k, carry):
            at = 8 * xr + k
            d1[j][at] = (d1[j][at].astype(F32) + r1[j, k].astype(F32)).astype(BF16)
            return carry

        lax.fori_loop(0, 8, add1, 0)
        for co in range(2):
            send(d1[j].at[pl.ds(8 * xr + 4 * co, 4)], rl1.at[col],
                 s2_s.at[j, 0, 0, co], s2_r.at[0, 0, col], (xr * 2 + co, m))
        arrived(r2.at[j], s1_s.at[j, 1], s1_r.at[j, 1])

        def add2(k, carry):
            at = 8 * xl + k
            d2[j][at] = (d2[j][at].astype(F32) + r2[j, k].astype(F32)).astype(BF16)
            return carry

        lax.fori_loop(0, 8, add2, 0)
        for co in range(2):
            send(d2[j].at[pl.ds(8 * xl + 4 * co, 4)], rr2.at[col],
                 s2_s.at[j, 1, 1, co], s2_r.at[1, 1, col], (xl * 2 + co, m))

    def finish(j):
        for cc, own in ((c, True), (o, False)):
            col = 3 * cc + j
            arrived(rr1.at[col], s2_s.at[j, 0, 1, 0], s2_r.at[0, 1, col])
            arrived(rl2.at[col], s2_s.at[j, 1, 0, 0], s2_r.at[1, 0, col])
            arrived(rl1.at[col], s2_s.at[j, 0, 0, 0], s2_r.at[0, 0, col])
            arrived(rr2.at[col], s2_s.at[j, 1, 1, 0], s2_r.at[1, 1, col])
            if not own:
                arrived(rp1.at[j], sp_s.at[j, 0], sp_r.at[j, 0])
                arrived(rp2.at[j], sp_s.at[j, 1], sp_r.at[j, 1])

            def body(k, carry):
                mine1 = d1[j][4 * s + k] if own else rp1[j, k]
                mine2 = d2[j][4 * s + k] if own else rp2[j, k]
                t1 = mine1.astype(F32) + rl1[col, k].astype(F32) + rr1[col, k].astype(F32)
                t2 = mine2.astype(F32) + rl2[col, k].astype(F32) + rr2[col, k].astype(F32)
                g1_out[col, k] = t1.T.astype(BF16)
                g2_out[col, k] = t2.astype(BF16)
                return carry

            lax.fori_loop(0, 4, body, 0)

    def group(ref, d, g):
        return ref.at[d, pl.ds(2 * g, 2)]

    def input_group(g):
        for d in D_ORDER:
            yy = (y + d) % NY

            def body(q, carry):
                zz = (z + q + 1) % NZ
                base = (yy * NZ + zz) * 3
                rows = []
                for t in range(3):
                    rows.append(
                        jnp.concatenate(
                            [w1[j][inv_sm[3 * c + j, base + t]] for j in range(COLS)], axis=1))
                rhs = jnp.concatenate(rows, axis=0)
                out = lax.dot_general(ghcat[...], rhs, NT, preferred_element_type=F32)
                dxo[d, q] = out[:128]
                pxs[d, q] = out[128:].astype(BF16)
                return carry

            lax.fori_loop(2 * g, 2 * g + 2, body, 0)
            send(group(pxs, d, g), group(prx, d, g), px_s.at[d, g], px_r.at[d, g], (x * 2 + o, m))

    def to_y(d, g):
        send(group(prx, d, g), yrc.at[d // 2, pl.ds(2 * g, 2)],
             y_s.at[d // 2, g], y_r.at[d // 2, g], (s, ((y + d) % NY) * NZ + z))

    def input_pair(g):
        step = 1 if g % 2 == 0 else 3
        for d in D_ORDER:
            arrived(group(prx, d, g), px_s.at[d, g], px_r.at[d, g])
            sent = d in (2, 4 - step)

            def body(q, carry):
                both = dxo[d, q] + prx[d, q].astype(F32)
                if sent:
                    prx[d, q] = both.astype(BF16)
                else:
                    dxo[d, q] = both
                return carry

            lax.fori_loop(2 * g, 2 * g + 2, body, 0)
            if d == 2:
                send(group(prx, 2, g), y1b.at[g], y1_s.at[g], y1_r.at[g],
                     (s, ((y + step) % NY) * NZ + z))
            elif sent:
                to_y(d, g)

    def input_added(g):
        d = 1 if g % 2 == 0 else 3
        arrived(y1b.at[g], y1_s.at[g], y1_r.at[g])
        for i in range(2):
            q = 2 * g + i
            prx[d, q] = (dxo[d, q] + y1b[g, i].astype(F32)).astype(BF16)
        to_y(d, g)

    def input_sum(g):
        for i in range(2):
            arrived(yrc.at[i, pl.ds(2 * g, 2)], y_s.at[i, g], y_r.at[i, g])
        for q in (2 * g, 2 * g + 1):
            both = dxo[0, q] + yrc[0, q].astype(F32) + yrc[1, q].astype(F32)
            if q < NZ - 1:
                zs[q] = both.astype(BF16)
                send(zs.at[q], zrc.at[q], z_s.at[q], z_r.at[q], at_z(q + 1))
            else:
                zown[...] = both

    def input_last():
        whole = zown[...]
        for q in range(NZ - 1):
            arrived(zrc.at[q], z_s.at[q], z_r.at[q])
            whole = whole + zrc[q].astype(F32)
        dx_out[...] = whole.astype(BF16)

    forward(0)
    forward(1)
    arrived(xf.at[pl.ds(0, 96), pl.ds(128, 128)], xs_s.at[0], xs_r.at[0])
    arrived(dyf.at[pl.ds(0, 96), pl.ds(128, 128)], xs_s.at[1], xs_r.at[1])
    pl.semaphore_wait(hello.at[1], 2)
    complete(0)
    forward_pass(0)
    forward(2)
    complete(1)
    forward_pass(1)
    weight_grads(0)
    weight_grads(1)
    complete(2)
    stage_one(0)
    stage_one(1)
    stage_two_plain(0)
    stage_two_plain(1)
    forward_pass(2)
    input_group(0)
    input_group(1)
    input_pair(0)
    input_group(2)
    input_pair(1)
    stage_two_added(0)
    input_group(3)
    input_added(0)
    input_pair(2)
    input_added(1)
    stage_two_added(1)
    input_pair(3)
    weight_grads(2)
    stage_one(2)
    stage_two_plain(2)
    input_sum(0)
    input_added(2)
    input_sum(1)
    input_added(3)
    stage_two_added(2)
    input_sum(2)
    input_sum(3)
    finish(0)
    finish(1)
    input_last()
    finish(2)
    for cp in pending:
        cp.wait_send()


def copy_out(dx, g1, g2, dx_out, g1_out, g2_out, sem):
    copies = [pltpu.make_async_copy(dx, dx_out, sem.at[12])]
    for col in range(6):
        copies.append(pltpu.make_async_copy(g1.at[col], g1_out.at[col], sem.at[2 * col]))
        copies.append(pltpu.make_async_copy(g2.at[col], g2_out.at[col], sem.at[2 * col + 1]))
    for cp in copies:
        cp.start()
    for cp in copies:
        cp.wait()


def per_device(inputs, out_grads, w1_blocks, w1_rows, w1_count, w2_blocks, w2_cols, w2_count):
    any_space = pl.BlockSpec(memory_space=pl.ANY)
    vmem = pl.BlockSpec(memory_space=pltpu.VMEM)
    smem = pl.BlockSpec(memory_space=pltpu.SMEM)
    dma = pltpu.SemaphoreType.DMA
    w_scratch = [pltpu.VMEM((33, 128, 128), BF16)] * 3 + [pltpu.VMEM((32, 128, 128), BF16)] * 3
    d_scratch = [pltpu.VMEM((32, 128, 128), BF16)] * 6
    shapes = (
        jax.ShapeDtypeStruct((128, 384), BF16),
        jax.ShapeDtypeStruct((6, 4, 128, 128), BF16),
        jax.ShapeDtypeStruct((6, 4, 128, 128), BF16),
    )
    grads = pl.pallas_call(
        kernel,
        out_shape=shapes,
        in_specs=[any_space] * 4 + [smem] * 4,
        out_specs=(vmem, vmem, vmem),
        scratch_shapes=[
            pltpu.VMEM((128, 12288), BF16),
            pltpu.VMEM((128, 12288), BF16),
            pltpu.VMEM((97, 256, 128), BF16),
            pltpu.VMEM((97, 256, 128), BF16),
            *w_scratch,
            pltpu.VMEM((16, 128), jnp.int32),
            pltpu.VMEM((8, 16, 128), jnp.int32),
            pltpu.VMEM((8, 128), jnp.int32),
            pltpu.SMEM((8, 16, 128), jnp.int32),
            pltpu.SMEM((8, 128), jnp.int32),
            pltpu.VMEM((256, 384), BF16),
            pltpu.VMEM((3, 128, 256), BF16),
            pltpu.VMEM((3, 128, 256), BF16),
            *d_scratch,
            pltpu.VMEM((3, 8, 128, 128), BF16),
            pltpu.VMEM((3, 8, 128, 128), BF16),
            pltpu.VMEM((6, 4, 128, 128), BF16),
            pltpu.VMEM((6, 4, 128, 128), BF16),
            pltpu.VMEM((6, 4, 128, 128), BF16),
            pltpu.VMEM((6, 4, 128, 128), BF16),
            pltpu.VMEM((3, 4, 128, 128), BF16),
            pltpu.VMEM((3, 4, 128, 128), BF16),
            pltpu.VMEM((4, 8, 128, 384), F32),
            pltpu.VMEM((4, 8, 128, 384), BF16),
            pltpu.VMEM((4, 8, 128, 384), BF16),
            pltpu.VMEM((4, 2, 128, 384), BF16),
            pltpu.VMEM((2, 8, 128, 384), BF16),
            pltpu.VMEM((7, 128, 384), BF16),
            pltpu.VMEM((128, 384), F32),
            pltpu.VMEM((7, 128, 384), BF16),
            pltpu.SemaphoreType.REGULAR((2,)),
            dma((11,)),
            dma((7,)), dma((7,)),
            dma((2,)), dma((2,)),
            dma((3, 2, 2, 2)), dma((3, 2, 2, 2)),
            dma((3, 2)), dma((3, 2)),
            dma((3, 2)), dma((3, 2)),
            dma((3, 2)), dma((3, 2)),
            dma((3, 2, 2, 2)), dma((2, 2, 6)),
            dma((3, 2)), dma((3, 2)),
            dma((4, 4)), dma((4, 4)),
            dma((4,)), dma((4,)),
            dma((2, 4)), dma((2, 4)),
            dma((7,)), dma((7,)),
        ],
        compiler_params=pltpu.CompilerParams(
            collective_id=0, has_side_effects=True, vmem_limit_bytes=60 * 1024 * 1024),
    )(inputs, out_grads, w1_blocks, w2_blocks, w1_rows.T, w1_count, w2_cols.T, w2_count)
    return pl.pallas_call(
        copy_out,
        out_shape=shapes,
        in_specs=[vmem] * 3,
        out_specs=(any_space,) * 3,
        scratch_shapes=[dma((13,))],
    )(*grads)


def solution(mesh):
    in_specs = (
        P("seq", None),
        P("seq", None),
        P("mp", "seq", None, None),
        P("mp", "seq"),
        P("mp"),
        P("mp", "seq", None, None),
        P("mp", "seq"),
        P("mp"),
    )
    out_specs = (P("seq", "mp"), P("mp", "seq", None, None), P("mp", "seq", None, None))
    return jax.shard_map(
        per_device, mesh=mesh, in_specs=in_specs, out_specs=out_specs, check_vma=False
    )
```

```python
import jax
import jax.numpy as jnp
from jax import lax
from jax.experimental import pallas as pl
from jax.experimental.pallas import tpu as pltpu
from jax.sharding import PartitionSpec as P

GELU_C = 0.7978845608028654
CUBIC = 0.044715
BF16 = jnp.bfloat16
F32 = jnp.float32
MESH = pl.DeviceIdType.MESH
NT = (((1,), (1,)), ((), ()))

NX = 4
NY = 4
NZ = 8
COLS = 3
D_ORDER = (2, 1, 3, 0)
PULLS = ((True, 0), (False, 0), (True, 1), (False, 1), (False, 2), (False, 3))


def gelu_both(h):
    arg = GELU_C * (h + CUBIC * h * h * h)
    t = jnp.tanh(arg)
    value = 0.5 * h * (1.0 + t)
    slope = 0.5 * (1.0 + t) + 0.5 * h * (1.0 - t * t) * GELU_C * (1.0 + 3.0 * CUBIC * h * h)
    return value, slope


def kernel(
    x_hbm, dy_hbm, w1_hbm, w2_hbm, rows_sm, count1_sm, cols_sm, count2_sm,
    dx_out, g1_out, g2_out,
    stx, sty, xf, dyf, dyp, w1a, w1b, w1c, w2a, w2b, w2c,
    pktv, idxv, tabv, tab_sm,
    hid, ag_own, ag_sent, ag_got, ghcat, ght, actt, actp,
    d1a, d1b, d1c, d2a, d2b, d2c,
    r1, rl1, rr1, rn2, rp1, rp2,
    dxo, pxs, prx, y1b, yrc, zs, zown, zrc,
    hello, loc_sem, pk_s, pk_r, xs_s, xs_r, wd_s, wd_r, wn_s, wn_r, wp_s, wp_r, wf_s, wf_r,
    pull_s, pull_r, ysh_s, ysh_r, zsh_s, zsh_r, rel_s, rel_r, ag_s, ag_r, ac_s, ac_r,
    s1_s, s1_r, s2_s, s2_r, sn_s, sn_r, sp_s, sp_r, px_s, px_r, y1_s, y1_r, y_s, y_r, z_s, z_r,
):
    w1 = (w1a, w1b, w1c)
    w2 = (w2a, w2b, w2c)
    d1 = (d1a, d1b, d1c)
    d2 = (d2a, d2b, d2c)
    s = lax.axis_index("seq")
    m = lax.axis_index("mp")
    x = s // 2
    c = s % 2
    o = 1 - c
    xl = (x + 3) % 4
    xr = (x + 1) % 4
    xo = (x + 2) % 4
    xp = x + 1 - 2 * (x % 2)
    xn = 3 - x
    y = m // NZ
    z = m % NZ
    zq = z % 4
    way_p = x % 2
    way_n = 1 - way_p
    pending = []

    def send(src, dst, ssem, rsem, dev):
        cp = pltpu.make_async_remote_copy(
            src_ref=src, dst_ref=dst, send_sem=ssem, recv_sem=rsem,
            device_id=dev, device_id_type=MESH,
        )
        cp.start()
        pending.append(cp)

    def arrived(ref, ssem, rsem):
        pltpu.make_async_remote_copy(
            src_ref=ref, dst_ref=ref, send_sem=ssem, recv_sem=rsem,
            device_id=(s, m), device_id_type=MESH,
        ).wait_recv()

    local = [
        pltpu.make_async_copy(x_hbm, stx, loc_sem.at[0]),
        pltpu.make_async_copy(dy_hbm, sty, loc_sem.at[1]),
    ]
    wlocal = []
    for j in range(COLS):
        wlocal.append(
            (
                pltpu.make_async_copy(
                    w1_hbm.at[3 * c + j], w1[j].at[pl.ds(4 * s, 4)], loc_sem.at[3 + 2 * j]),
                pltpu.make_async_copy(
                    w2_hbm.at[3 * c + j], w2[j].at[pl.ds(4 * c, 4)], loc_sem.at[4 + 2 * j]),
            )
        )
    for cp in local:
        cp.start()
    for pair in wlocal:
        for cp in pair:
            cp.start()

    def at_z(e):
        return (s, y * NZ + (z + e) % NZ)

    barrier = pltpu.get_barrier_semaphore()
    for e in range(1, 8):
        pl.semaphore_signal(barrier, inc=1, device_id=((s + e) % 8, m), device_id_type=MESH)
    for e in range(1, NY):
        pl.semaphore_signal(
            barrier, inc=1, device_id=(s, ((y + e) % NY) * NZ + z), device_id_type=MESH)
    for e in (1, NZ - 1):
        pl.semaphore_signal(barrier, inc=1, device_id=at_z(e), device_id_type=MESH)

    sub = lax.broadcasted_iota(jnp.int32, (8, 128), 0)
    lane = lax.broadcasted_iota(jnp.int32, (8, 128), 1)
    named = jnp.zeros((8, 128), jnp.int32)
    slot_of = jnp.zeros((8, 128), jnp.int32)
    for col in range(6):
        for k in range(4):
            slot = 4 * s + k
            row = jnp.where(slot < count1_sm[col], rows_sm[k, col], 96)
            other = jnp.where(slot < count2_sm[col], cols_sm[k, col], 96)
            named = jnp.where((sub == col) & (lane == 8 * s + k), row, named)
            named = jnp.where((sub == col) & (lane == 8 * s + 4 + k), other, named)
            slot_of = jnp.where((sub == col) & (lane == row), slot + 1, slot_of)
    pktv[0:8] = named
    pktv[8:16] = slot_of

    def regrouped(at, flat, full):
        local[at].wait()

        def body(r, carry):
            full[r, 0:128] = flat[:, pl.ds(pl.multiple_of(r * 128, 128), 128)]
            return carry

        lax.fori_loop(0, 96, body, 0, unroll=8)
        full[96] = jnp.zeros((256, 128), BF16)

    pl.semaphore_wait(barrier, 7 + NY - 1 + 2)

    pulls = []

    def pull():
        n = len(pulls)
        along_z, i = PULLS[n]
        first = 64 + 8 * zq + 4 * i if along_z else 16 * y + 4 * i
        send(dyf.at[pl.ds(first, 4), pl.ds(0, 128)], dyp.at[pl.ds(first, 4), pl.ds(0, 128)],
             pull_s.at[n], pull_r.at[n], (xp * 2 + c, m))
        pulls.append(pending.pop())

    def next_pull():
        pulls[len(pulls) - 2].wait_send()
        pull()

    for e in range(1, 8):
        send(pktv, idxv.at[s], pk_s.at[e - 1], pk_r.at[e - 1], ((s + e) % 8, m))
    idxv[s] = pktv[...]
    for e in (1, NZ - 1):
        pl.semaphore_signal(hello.at[0], inc=1, device_id=at_z(e), device_id_type=MESH)

    def direct_one(j, xd, way):
        for cd in range(2):
            send(w1_hbm.at[3 * cd + j], w1[j].at[pl.ds(4 * s, 4)],
                 wd_s.at[j, way, cd], wd_r.at[j, way, c], (xd * 2 + cd, m))

    def core_one(j):
        send(w1_hbm.at[3 * o + j], w1[j].at[pl.ds(4 * s, 4)],
             wp_s.at[j, 0], wp_r.at[j, 0], (x * 2 + o, m))

    def direct_two(j):
        for cd in range(2):
            send(w2_hbm.at[3 * cd + j], w2[j].at[pl.ds(8 + 4 * c, 4)],
                 wn_s.at[j, cd], wn_r.at[j, c], (xn * 2 + cd, m))
        send(w2_hbm.at[3 * o + j], w2[j].at[pl.ds(4 * c, 4)],
             wp_s.at[j, 1], wp_r.at[j, 1], (x * 2 + o, m))

    def from_chip(j, xs, way, cs):
        arrived(w1[j].at[pl.ds(8 * xs + 4 * cs, 4)], wd_s.at[j, way, cs], wd_r.at[j, way, cs])

    def forward(j, xs, xd, way):
        from_chip(j, xs, way, way)
        part = w1[j].at[pl.ds(8 * xs + 4 * way, 4)]
        send(part, part, wf_s.at[j, way], wf_r.at[j, way], (xd * 2 + c, m))

    def complete_one(j):
        wlocal[j][0].wait()
        arrived(w1[j].at[pl.ds(8 * x + 4 * o, 4)], wp_s.at[j, 0], wp_r.at[j, 0])
        from_chip(j, xn, way_p, 1 - way_p)
        from_chip(j, xp, way_n, 1 - way_n)
        for way in range(2):
            arrived(w1[j].at[pl.ds(8 * xo + 4 * way, 4)], wf_s.at[j, way], wf_r.at[j, way])

    def complete_two(j):
        wlocal[j][1].wait()
        arrived(w2[j].at[pl.ds(4 * o, 4)], wp_s.at[j, 1], wp_r.at[j, 1])
        for cs in range(2):
            arrived(w2[j].at[pl.ds(8 + 4 * cs, 4)], wn_s.at[j, cs], wn_r.at[j, cs])

    for j in range(COLS):
        direct_one(j, xn, way_n)

    def to_core(at, full):
        send(full.at[pl.ds(0, 96), pl.ds(0, 128)], full.at[pl.ds(0, 96), pl.ds(128, 128)],
             xs_s.at[at], xs_r.at[at], (x * 2 + o, m))

    regrouped(1, sty, dyf)
    pull()
    pull()
    for j in range(COLS):
        core_one(j)
    regrouped(0, stx, xf)
    to_core(1, dyf)
    next_pull()
    dyp[96] = jnp.zeros((256, 128), BF16)

    for j in range(COLS):
        w1[j][32] = jnp.zeros((128, 128), BF16)

    pl.semaphore_wait(hello.at[0], 2)
    for e in (2, NZ - 2):
        pl.semaphore_signal(hello.at[1], inc=1, device_id=at_z(e), device_id_type=MESH)

    def part_of(first, half):
        return dyp.at[pl.ds(first, 4), pl.ds(128 * half, 128)]

    def relay(n, first):
        send(part_of(first, 0), part_of(first, 1), rel_s.at[n], rel_r.at[n], (x * 2 + o, m))

    def y_first(e, i):
        return 16 * ((y + 4 - e) % 4) + 4 * i

    def z_first(e, i):
        return 64 + 8 * ((zq + 4 - e) % 4) + 4 * i

    def share(n):
        along_z, i = PULLS[n]
        first = z_first(0, i) if along_z else y_first(0, i)
        arrived(part_of(first, 0), pull_s.at[n], pull_r.at[n])
        for e in (1, 3, 2):
            if along_z:
                send(part_of(first, 0), part_of(first, 0), zsh_s.at[e - 1, i], zsh_r.at[e - 1, i],
                     (s, y * NZ + z - zq + (zq + e) % 4))
            else:
                send(part_of(first, 0), part_of(first, 0), ysh_s.at[e - 1, i], ysh_r.at[e - 1, i],
                     (s, ((y + e) % NY) * NZ + z))
        relay(n, first)

    def relay_y(i):
        for e in range(1, 4):
            arrived(part_of(y_first(e, i), 0), ysh_s.at[e - 1, i], ysh_r.at[e - 1, i])
            relay(6 + 4 * (e - 1) + i, y_first(e, i))

    def relay_z(i):
        for e in range(1, 4):
            arrived(part_of(z_first(e, i), 0), zsh_s.at[e - 1, i], zsh_r.at[e - 1, i])
            relay(18 + 2 * (e - 1) + i, z_first(e, i))

    def partner_ready():
        for n, (along_z, i) in enumerate(PULLS):
            first = z_first(0, i) if along_z else y_first(0, i)
            arrived(part_of(first, 1), rel_s.at[n], rel_r.at[n])
        for e in range(1, 4):
            for i in range(4):
                n = 6 + 4 * (e - 1) + i
                arrived(part_of(y_first(e, i), 1), rel_s.at[n], rel_r.at[n])
            for i in range(2):
                n = 18 + 2 * (e - 1) + i
                arrived(part_of(z_first(e, i), 1), rel_s.at[n], rel_r.at[n])

    for e in range(1, 8):
        arrived(idxv.at[(s + 8 - e) % 8], pk_s.at[e - 1], pk_r.at[e - 1])
    total = idxv[0]
    for t in range(1, 8):
        total = total + idxv[t]
    tabv[0:8] = total[0:8]
    tabv[8:16] = jnp.where(total[8:16] > 0, total[8:16] - 1, 32)
    to_sm = pltpu.make_async_copy(tabv, tab_sm, loc_sem.at[9])
    to_sm.start()
    to_sm.wait()

    def picked(ref, who, col, first):
        return jnp.concatenate([ref[tab_sm[col, 8 * who + first + u]] for u in range(4)], axis=1)

    def owner(p):
        other = p // 2
        return 2 * (x + other * (xn - x)) + p % 2

    def hidden_pass(j):
        col = 3 * c + j

        def body(p, h):
            xs = picked(xf, p, col, 0)
            ws = w1[j][pl.ds(4 * p, 4)].reshape(512, 128)
            return h + jnp.dot(xs, ws, preferred_element_type=F32)

        hid[j] = lax.fori_loop(0, 8, body, jnp.zeros((256, 128), F32))

    def act_grads(j, full):
        col = 3 * c + j

        def body(p, a):
            vs = jnp.concatenate([w2[j][4 * p + u] for u in range(4)], axis=1)
            ys = picked(full, owner(p), col, 4)
            return a + lax.dot_general(ys, vs, NT, preferred_element_type=F32)

        return lax.fori_loop(0, 4, body, jnp.zeros((256, 128), F32))

    def act_own(j):
        ag_own[j] = act_grads(j, dyf)

    def act_other(j):
        ag_sent[j] = act_grads(j, dyp).astype(BF16)
        send(ag_sent.at[j], ag_got.at[j], ag_s.at[j], ag_r.at[j], (xp * 2 + c, m))

    def activate(j):
        value, slope = gelu_both(hid[j])
        hid[j] = slope
        actt[j] = value.T.astype(BF16)
        send(actt.at[j], actp.at[j], ac_s.at[j], ac_r.at[j], (xp * 2 + c, m))

    def hidden_grads(j):
        arrived(ag_got.at[j], ag_s.at[j], ag_r.at[j])
        grad = (ag_own[j] + ag_got[j].astype(F32)) * hid[j]
        ghcat[:, j * 128:(j + 1) * 128] = grad.astype(BF16)
        ght[j] = grad.T.astype(BF16)

    def grads_one(j):
        col = 3 * c + j

        def body(q, carry):
            who = (2 * xo + q) % 8
            t1 = jnp.dot(ght[j], picked(xf, who, col, 0), preferred_element_type=F32)
            for u in range(4):
                d1[j][4 * who + u] = t1[:, 128 * u:128 * (u + 1)].astype(BF16)
            return carry

        lax.fori_loop(0, 8, body, 0)
        send(d1[j].at[pl.ds(8 * xo, 4)], r1.at[j, pl.ds(0, 4)],
             s1_s.at[j, 0], s1_r.at[j, 0], (xr * 2 + c, m))
        send(d1[j].at[pl.ds(8 * xo + 4, 4)], r1.at[j, pl.ds(4, 4)],
             s1_s.at[j, 1], s1_r.at[j, 1], (xl * 2 + c, m))
        send(d1[j].at[pl.ds(8 * xr + 4, 4)], rl1.at[col],
             s2_s.at[j, 0, 1], s2_r.at[0, col], (xr * 2 + 1, m))
        send(d1[j].at[pl.ds(8 * xl, 4)], rr1.at[col],
             s2_s.at[j, 1, 0], s2_r.at[1, col], (xl * 2, m))
        send(d1[j].at[pl.ds(8 * x + 4 * o, 4)], rp1.at[j], sp_s.at[j, 0], sp_r.at[j, 0], (x * 2 + o, m))

    def grads_two(j):
        col = 3 * c + j
        arrived(actp.at[j], ac_s.at[j], ac_r.at[j])

        def body(p, carry):
            t2 = jnp.dot(actt[j], picked(dyf, owner(p), col, 4), preferred_element_type=F32)
            t2 = t2 + jnp.dot(actp[j], picked(dyp, owner(p), col, 4), preferred_element_type=F32)
            for u in range(4):
                d2[j][4 * p + u] = t2[:, 128 * u:128 * (u + 1)].astype(BF16)
            return carry

        lax.fori_loop(0, 4, body, 0)
        for co in range(2):
            send(d2[j].at[pl.ds(8 + 4 * co, 4)], rn2.at[col],
                 sn_s.at[j, co], sn_r.at[col], (xn * 2 + co, m))
        send(d2[j].at[pl.ds(4 * o, 4)], rp2.at[j], sp_s.at[j, 1], sp_r.at[j, 1], (x * 2 + o, m))

    def grads_added(j):
        col = 3 * c + j
        for way, xd, into in ((0, xr, rl1), (1, xl, rr1)):
            arrived(r1.at[j, pl.ds(4 * way, 4)], s1_s.at[j, way], s1_r.at[j, way])

            def body(k, carry):
                at = 8 * xd + 4 * way + k
                d1[j][at] = (d1[j][at].astype(F32) + r1[j, 4 * way + k].astype(F32)).astype(BF16)
                return carry

            lax.fori_loop(0, 4, body, 0)
            send(d1[j].at[pl.ds(8 * xd + 4 * way, 4)], into.at[col],
                 s2_s.at[j, way, way], s2_r.at[way, col], (xd * 2 + way, m))

    def finish(j):
        for cc, own in ((c, True), (o, False)):
            col = 3 * cc + j
            arrived(rn2.at[col], sn_s.at[j, 0], sn_r.at[col])
            arrived(rl1.at[col], s2_s.at[j, 0, 0], s2_r.at[0, col])
            arrived(rr1.at[col], s2_s.at[j, 1, 0], s2_r.at[1, col])
            if not own:
                arrived(rp1.at[j], sp_s.at[j, 0], sp_r.at[j, 0])
                arrived(rp2.at[j], sp_s.at[j, 1], sp_r.at[j, 1])

            def body(k, carry):
                mine1 = d1[j][4 * s + k] if own else rp1[j, k]
                mine2 = d2[j][4 * c + k] if own else rp2[j, k]
                t1 = mine1.astype(F32) + rl1[col, k].astype(F32) + rr1[col, k].astype(F32)
                t2 = mine2.astype(F32) + rn2[col, k].astype(F32)
                g1_out[col, k] = t1.T.astype(BF16)
                g2_out[col, k] = t2.astype(BF16)
                return carry

            lax.fori_loop(0, 4, body, 0)

    def group(ref, d, g):
        return ref.at[d, pl.ds(2 * g, 2)]

    def input_group(g):
        for d in D_ORDER:
            yy = (y + d) % NY

            def body(q, carry):
                zz = (z + q + 1) % NZ
                base = (yy * NZ + zz) * 3
                rows = []
                for t in range(3):
                    rows.append(
                        jnp.concatenate(
                            [w1[j][tab_sm[8 + 3 * c + j, base + t]] for j in range(COLS)], axis=1))
                rhs = jnp.concatenate(rows, axis=0)
                out = lax.dot_general(ghcat[...], rhs, NT, preferred_element_type=F32)
                dxo[d, q] = out[:128]
                pxs[d, q] = out[128:].astype(BF16)
                return carry

            lax.fori_loop(2 * g, 2 * g + 2, body, 0)
            send(group(pxs, d, g), group(prx, d, g), px_s.at[d, g], px_r.at[d, g], (x * 2 + o, m))

    def to_y(d, g):
        send(group(prx, d, g), yrc.at[d // 2, pl.ds(2 * g, 2)],
             y_s.at[d // 2, g], y_r.at[d // 2, g], (s, ((y + d) % NY) * NZ + z))

    def input_pair(g):
        step = 1 if g % 2 == 0 else 3
        for d in D_ORDER:
            arrived(group(prx, d, g), px_s.at[d, g], px_r.at[d, g])
            sent = d in (2, 4 - step)

            def body(q, carry):
                both = dxo[d, q] + prx[d, q].astype(F32)
                if sent:
                    prx[d, q] = both.astype(BF16)
                else:
                    dxo[d, q] = both
                return carry

            lax.fori_loop(2 * g, 2 * g + 2, body, 0)
            if d == 2:
                send(group(prx, 2, g), y1b.at[g], y1_s.at[g], y1_r.at[g],
                     (s, ((y + step) % NY) * NZ + z))
            elif sent:
                to_y(d, g)

    def input_added(g):
        d = 1 if g % 2 == 0 else 3
        arrived(y1b.at[g], y1_s.at[g], y1_r.at[g])
        for i in range(2):
            q = 2 * g + i
            prx[d, q] = (dxo[d, q] + y1b[g, i].astype(F32)).astype(BF16)
        to_y(d, g)

    def input_sum(g):
        for i in range(2):
            arrived(yrc.at[i, pl.ds(2 * g, 2)], y_s.at[i, g], y_r.at[i, g])
        for q in (2 * g, 2 * g + 1):
            both = dxo[0, q] + yrc[0, q].astype(F32) + yrc[1, q].astype(F32)
            if q < NZ - 1:
                zs[q] = both.astype(BF16)
                send(zs.at[q], zrc.at[q], z_s.at[q], z_r.at[q], at_z(q + 1))
            else:
                zown[...] = both

    def input_last():
        whole = zown[...]
        for q in range(NZ - 1):
            arrived(zrc.at[q], z_s.at[q], z_r.at[q])
            whole = whole + zrc[q].astype(F32)
        dx_out[...] = whole.astype(BF16)

    pl.semaphore_wait(hello.at[1], 2)
    share(0)
    next_pull()
    share(1)
    next_pull()
    share(2)
    next_pull()
    direct_two(0)
    share(3)
    direct_two(1)
    direct_one(0, xp, way_p)
    share(4)
    direct_two(2)
    direct_one(1, xp, way_p)
    share(5)
    direct_one(2, xp, way_p)
    forward(0, xn, xp, way_p)
    forward(1, xn, xp, way_p)
    forward(2, xn, xp, way_p)
    to_core(0, xf)
    relay_z(0)
    relay_y(0)
    forward(0, xp, xn, way_n)
    arrived(dyf.at[pl.ds(0, 96), pl.ds(128, 128)], xs_s.at[1], xs_r.at[1])
    arrived(xf.at[pl.ds(0, 96), pl.ds(128, 128)], xs_s.at[0], xs_r.at[0])
    relay_z(1)
    relay_y(1)
    forward(1, xp, xn, way_n)
    relay_y(2)
    complete_two(0)
    act_own(0)
    relay_y(3)
    forward(2, xp, xn, way_n)
    complete_two(1)
    complete_two(2)
    partner_ready()
    act_other(0)
    act_other(1)
    act_other(2)
    act_own(1)
    act_own(2)
    complete_one(0)
    hidden_pass(0)
    activate(0)
    hidden_grads(0)
    complete_one(1)
    hidden_pass(1)
    activate(1)
    hidden_grads(1)
    grads_one(0)
    complete_one(2)
    hidden_pass(2)
    activate(2)
    hidden_grads(2)
    input_group(0)
    grads_two(0)
    input_group(1)
    input_pair(0)
    grads_one(1)
    input_group(2)
    input_pair(1)
    input_added(0)
    grads_two(1)
    grads_added(0)
    input_group(3)
    input_pair(2)
    input_added(1)
    input_sum(0)
    input_pair(3)
    grads_one(2)
    grads_added(1)
    input_added(2)
    input_sum(1)
    grads_two(2)
    input_added(3)
    grads_added(2)
    input_sum(2)
    finish(0)
    input_sum(3)
    finish(1)
    input_last()
    finish(2)
    for cp in pending + pulls[-2:]:
        cp.wait_send()


def copy_out(dx, g1, g2, dx_out, g1_out, g2_out, sem):
    copies = [pltpu.make_async_copy(dx, dx_out, sem.at[12])]
    for col in range(6):
        copies.append(pltpu.make_async_copy(g1.at[col], g1_out.at[col], sem.at[2 * col]))
        copies.append(pltpu.make_async_copy(g2.at[col], g2_out.at[col], sem.at[2 * col + 1]))
    for cp in copies:
        cp.start()
    for cp in copies:
        cp.wait()


def per_device(inputs, out_grads, w1_blocks, w1_rows, w1_count, w2_blocks, w2_cols, w2_count):
    any_space = pl.BlockSpec(memory_space=pl.ANY)
    vmem = pl.BlockSpec(memory_space=pltpu.VMEM)
    smem = pl.BlockSpec(memory_space=pltpu.SMEM)
    dma = pltpu.SemaphoreType.DMA
    w_scratch = [pltpu.VMEM((33, 128, 128), BF16)] * 3 + [pltpu.VMEM((16, 128, 128), BF16)] * 3
    d_scratch = [pltpu.VMEM((32, 128, 128), BF16)] * 3 + [pltpu.VMEM((16, 128, 128), BF16)] * 3
    shapes = (
        jax.ShapeDtypeStruct((128, 384), BF16),
        jax.ShapeDtypeStruct((6, 4, 128, 128), BF16),
        jax.ShapeDtypeStruct((6, 4, 128, 128), BF16),
    )
    grads = pl.pallas_call(
        kernel,
        out_shape=shapes,
        in_specs=[any_space] * 4 + [smem] * 4,
        out_specs=(vmem, vmem, vmem),
        scratch_shapes=[
            pltpu.VMEM((128, 12288), BF16),
            pltpu.VMEM((128, 12288), BF16),
            pltpu.VMEM((97, 256, 128), BF16),
            pltpu.VMEM((97, 256, 128), BF16),
            pltpu.VMEM((97, 256, 128), BF16),
            *w_scratch,
            pltpu.VMEM((16, 128), jnp.int32),
            pltpu.VMEM((8, 16, 128), jnp.int32),
            pltpu.VMEM((16, 128), jnp.int32),
            pltpu.SMEM((16, 128), jnp.int32),
            *[pltpu.VMEM((3, 256, 128), F32)] * 2,
            *[pltpu.VMEM((3, 256, 128), BF16)] * 2,
            pltpu.VMEM((256, 384), BF16),
            *[pltpu.VMEM((3, 128, 256), BF16)] * 3,
            *d_scratch,
            pltpu.VMEM((3, 8, 128, 128), BF16),
            pltpu.VMEM((6, 4, 128, 128), BF16),
            pltpu.VMEM((6, 4, 128, 128), BF16),
            pltpu.VMEM((6, 4, 128, 128), BF16),
            pltpu.VMEM((3, 4, 128, 128), BF16),
            pltpu.VMEM((3, 4, 128, 128), BF16),
            pltpu.VMEM((4, 8, 128, 384), F32),
            pltpu.VMEM((4, 8, 128, 384), BF16),
            pltpu.VMEM((4, 8, 128, 384), BF16),
            pltpu.VMEM((4, 2, 128, 384), BF16),
            pltpu.VMEM((2, 8, 128, 384), BF16),
            pltpu.VMEM((7, 128, 384), BF16),
            pltpu.VMEM((128, 384), F32),
            pltpu.VMEM((7, 128, 384), BF16),
            pltpu.SemaphoreType.REGULAR((2,)),
            dma((11,)),
            dma((7,)), dma((7,)),
            dma((2,)), dma((2,)),
            dma((3, 2, 2)), dma((3, 2, 2)),
            dma((3, 2)), dma((3, 2)),
            dma((3, 2)), dma((3, 2)),
            dma((3, 2)), dma((3, 2)),
            dma((6,)), dma((6,)),
            dma((3, 4)), dma((3, 4)),
            dma((3, 2)), dma((3, 2)),
            dma((24,)), dma((24,)),
            dma((3,)), dma((3,)),
            dma((3,)), dma((3,)),
            dma((3, 2)), dma((3, 2)),
            dma((3, 2, 2)), dma((2, 6)),
            dma((3, 2)), dma((6,)),
            dma((3, 2)), dma((3, 2)),
            dma((4, 4)), dma((4, 4)),
            dma((4,)), dma((4,)),
            dma((2, 4)), dma((2, 4)),
            dma((7,)), dma((7,)),
        ],
        compiler_params=pltpu.CompilerParams(
            collective_id=0, has_side_effects=True, vmem_limit_bytes=60 * 1024 * 1024),
    )(inputs, out_grads, w1_blocks, w2_blocks, w1_rows.T, w1_count, w2_cols.T, w2_count)
    return pl.pallas_call(
        copy_out,
        out_shape=shapes,
        in_specs=[vmem] * 3,
        out_specs=(any_space,) * 3,
        scratch_shapes=[dma((13,))],
    )(*grads)


def solution(mesh):
    in_specs = (
        P("seq", None),
        P("seq", None),
        P("mp", "seq", None, None),
        P("mp", "seq"),
        P("mp"),
        P("mp", "seq", None, None),
        P("mp", "seq"),
        P("mp"),
    )
    out_specs = (P("seq", "mp"), P("mp", "seq", None, None), P("mp", "seq", None, None))
    return jax.shard_map(
        per_device, mesh=mesh, in_specs=in_specs, out_specs=out_specs, check_vma=False
    )
```

```python
import jax
import jax.numpy as jnp
from jax import lax
from jax.experimental import pallas as pl
from jax.experimental.pallas import tpu as pltpu
from jax.sharding import PartitionSpec as P

GELU_C = 0.7978845608028654
CUBIC = 0.044715
BF16 = jnp.bfloat16
F32 = jnp.float32
MESH = pl.DeviceIdType.MESH
NT = (((1,), (1,)), ((), ()))

NX = 4
NY = 4
NZ = 8
COLS = 3
D_ORDER = (2, 1, 3, 0)
PULLS = ((True, 0), (False, 0), (True, 1), (False, 1), (False, 2), (False, 3))


def gelu_both(h):
    arg = GELU_C * (h + CUBIC * h * h * h)
    t = jnp.tanh(arg)
    value = 0.5 * h * (1.0 + t)
    slope = 0.5 * (1.0 + t) + 0.5 * h * (1.0 - t * t) * GELU_C * (1.0 + 3.0 * CUBIC * h * h)
    return value, slope


def kernel(
    x_hbm, dy_hbm, w1_hbm, w2_hbm, rows_sm, count1_sm, cols_sm, count2_sm,
    dx_out, g1_hbm, g2_hbm,
    stx, sty, xf, dyf, dyp, w1a, w1b, w1c, w2a, w2b, w2c,
    pktv, idxv, tabv, tab_sm,
    hid, ag_own, ag_sent, ag_got, ghcat, ght, actt, actp,
    d1a, d1b, d1c, d2a, d2b, d2c,
    r1, rl1, rr1, rn2, rp1, rp2,
    g1_out, g2_out, dxo, pxs, prx, y1b, yrc, zs, zown, zrc,
    out_sem, hello, loc_sem, pk_s, pk_r, xs_s, xs_r, wd_s, wd_r, wn_s, wn_r, wp_s, wp_r, wf_s, wf_r,
    pull_s, pull_r, ysh_s, ysh_r, zsh_s, zsh_r, rel_s, rel_r, ag_s, ag_r, ac_s, ac_r,
    s1_s, s1_r, s2_s, s2_r, sn_s, sn_r, sp_s, sp_r, px_s, px_r, y1_s, y1_r, y_s, y_r, z_s, z_r,
):
    w1 = (w1a, w1b, w1c)
    w2 = (w2a, w2b, w2c)
    d1 = (d1a, d1b, d1c)
    d2 = (d2a, d2b, d2c)
    s = lax.axis_index("seq")
    m = lax.axis_index("mp")
    x = s // 2
    c = s % 2
    o = 1 - c
    xl = (x + 3) % 4
    xr = (x + 1) % 4
    xo = (x + 2) % 4
    xp = x + 1 - 2 * (x % 2)
    xn = 3 - x
    y = m // NZ
    z = m % NZ
    zq = z % 4
    way_p = x % 2
    way_n = 1 - way_p
    pending = []
    leaving = []

    def send(src, dst, ssem, rsem, dev):
        cp = pltpu.make_async_remote_copy(
            src_ref=src, dst_ref=dst, send_sem=ssem, recv_sem=rsem,
            device_id=dev, device_id_type=MESH,
        )
        cp.start()
        pending.append(cp)

    def arrived(ref, ssem, rsem):
        pltpu.make_async_remote_copy(
            src_ref=ref, dst_ref=ref, send_sem=ssem, recv_sem=rsem,
            device_id=(s, m), device_id_type=MESH,
        ).wait_recv()

    local = [
        pltpu.make_async_copy(x_hbm, stx, loc_sem.at[0]),
        pltpu.make_async_copy(dy_hbm, sty, loc_sem.at[1]),
    ]
    wlocal = []
    for j in range(COLS):
        wlocal.append(
            (
                pltpu.make_async_copy(
                    w1_hbm.at[3 * c + j], w1[j].at[pl.ds(4 * s, 4)], loc_sem.at[3 + 2 * j]),
                pltpu.make_async_copy(
                    w2_hbm.at[3 * c + j], w2[j].at[pl.ds(4 * c, 4)], loc_sem.at[4 + 2 * j]),
            )
        )
    for cp in local:
        cp.start()
    for pair in wlocal:
        for cp in pair:
            cp.start()

    def at_z(e):
        return (s, y * NZ + (z + e) % NZ)

    barrier = pltpu.get_barrier_semaphore()
    for e in range(1, 8):
        pl.semaphore_signal(barrier, inc=1, device_id=((s + e) % 8, m), device_id_type=MESH)
    for e in range(1, NY):
        pl.semaphore_signal(
            barrier, inc=1, device_id=(s, ((y + e) % NY) * NZ + z), device_id_type=MESH)
    for e in (1, NZ - 1):
        pl.semaphore_signal(barrier, inc=1, device_id=at_z(e), device_id_type=MESH)

    sub = lax.broadcasted_iota(jnp.int32, (8, 128), 0)
    lane = lax.broadcasted_iota(jnp.int32, (8, 128), 1)
    named = jnp.zeros((8, 128), jnp.int32)
    slot_of = jnp.zeros((8, 128), jnp.int32)
    for col in range(6):
        for k in range(4):
            slot = 4 * s + k
            row = jnp.where(slot < count1_sm[col], rows_sm[k, col], 96)
            other = jnp.where(slot < count2_sm[col], cols_sm[k, col], 96)
            named = jnp.where((sub == col) & (lane == 8 * s + k), row, named)
            named = jnp.where((sub == col) & (lane == 8 * s + 4 + k), other, named)
            slot_of = jnp.where((sub == col) & (lane == row), slot + 1, slot_of)
    pktv[0:8] = named
    pktv[8:16] = slot_of

    def regrouped(at, flat, full):
        local[at].wait()

        def body(r, carry):
            full[r, 0:128] = flat[:, pl.ds(pl.multiple_of(r * 128, 128), 128)]
            return carry

        lax.fori_loop(0, 96, body, 0, unroll=8)
        full[96] = jnp.zeros((256, 128), BF16)

    pl.semaphore_wait(barrier, 7 + NY - 1 + 2)

    pulls = []

    def pull():
        n = len(pulls)
        along_z, i = PULLS[n]
        first = 64 + 8 * zq + 4 * i if along_z else 16 * y + 4 * i
        send(dyf.at[pl.ds(first, 4), pl.ds(0, 128)], dyp.at[pl.ds(first, 4), pl.ds(0, 128)],
             pull_s.at[n], pull_r.at[n], (xp * 2 + c, m))
        pulls.append(pending.pop())

    def next_pull():
        pulls[len(pulls) - 2].wait_send()
        pull()

    for e in range(1, 8):
        send(pktv, idxv.at[s], pk_s.at[e - 1], pk_r.at[e - 1], ((s + e) % 8, m))
    idxv[s] = pktv[...]
    for e in (1, NZ - 1):
        pl.semaphore_signal(hello.at[0], inc=1, device_id=at_z(e), device_id_type=MESH)

    def direct_one(j, xd, way):
        for cd in range(2):
            send(w1_hbm.at[3 * cd + j], w1[j].at[pl.ds(4 * s, 4)],
                 wd_s.at[j, way, cd], wd_r.at[j, way, c], (xd * 2 + cd, m))

    def core_one(j):
        send(w1_hbm.at[3 * o + j], w1[j].at[pl.ds(4 * s, 4)],
             wp_s.at[j, 0], wp_r.at[j, 0], (x * 2 + o, m))

    def direct_two(j):
        for cd in range(2):
            send(w2_hbm.at[3 * cd + j], w2[j].at[pl.ds(8 + 4 * c, 4)],
                 wn_s.at[j, cd], wn_r.at[j, c], (xn * 2 + cd, m))
        send(w2_hbm.at[3 * o + j], w2[j].at[pl.ds(4 * c, 4)],
             wp_s.at[j, 1], wp_r.at[j, 1], (x * 2 + o, m))

    def from_chip(j, xs, way, cs):
        arrived(w1[j].at[pl.ds(8 * xs + 4 * cs, 4)], wd_s.at[j, way, cs], wd_r.at[j, way, cs])

    def forward(j, xs, xd, way):
        from_chip(j, xs, way, way)
        part = w1[j].at[pl.ds(8 * xs + 4 * way, 4)]
        send(part, part, wf_s.at[j, way], wf_r.at[j, way], (xd * 2 + c, m))

    def complete_one(j):
        wlocal[j][0].wait()
        arrived(w1[j].at[pl.ds(8 * x + 4 * o, 4)], wp_s.at[j, 0], wp_r.at[j, 0])
        from_chip(j, xn, way_p, 1 - way_p)
        from_chip(j, xp, way_n, 1 - way_n)
        for way in range(2):
            arrived(w1[j].at[pl.ds(8 * xo + 4 * way, 4)], wf_s.at[j, way], wf_r.at[j, way])

    def complete_two(j):
        wlocal[j][1].wait()
        arrived(w2[j].at[pl.ds(4 * o, 4)], wp_s.at[j, 1], wp_r.at[j, 1])
        for cs in range(2):
            arrived(w2[j].at[pl.ds(8 + 4 * cs, 4)], wn_s.at[j, cs], wn_r.at[j, cs])

    for j in range(COLS):
        direct_one(j, xn, way_n)

    def to_core(at, full):
        send(full.at[pl.ds(0, 96), pl.ds(0, 128)], full.at[pl.ds(0, 96), pl.ds(128, 128)],
             xs_s.at[at], xs_r.at[at], (x * 2 + o, m))

    regrouped(1, sty, dyf)
    pull()
    pull()
    for j in range(COLS):
        core_one(j)
    regrouped(0, stx, xf)
    to_core(1, dyf)
    next_pull()
    dyp[96] = jnp.zeros((256, 128), BF16)

    for j in range(COLS):
        w1[j][32] = jnp.zeros((128, 128), BF16)

    pl.semaphore_wait(hello.at[0], 2)
    for e in (2, NZ - 2):
        pl.semaphore_signal(hello.at[1], inc=1, device_id=at_z(e), device_id_type=MESH)

    def part_of(first, half):
        return dyp.at[pl.ds(first, 4), pl.ds(128 * half, 128)]

    def relay(n, first):
        send(part_of(first, 0), part_of(first, 1), rel_s.at[n], rel_r.at[n], (x * 2 + o, m))

    def y_first(e, i):
        return 16 * ((y + 4 - e) % 4) + 4 * i

    def z_first(e, i):
        return 64 + 8 * ((zq + 4 - e) % 4) + 4 * i

    def share(n):
        along_z, i = PULLS[n]
        first = z_first(0, i) if along_z else y_first(0, i)
        arrived(part_of(first, 0), pull_s.at[n], pull_r.at[n])
        for e in (1, 3, 2):
            if along_z:
                send(part_of(first, 0), part_of(first, 0), zsh_s.at[e - 1, i], zsh_r.at[e - 1, i],
                     (s, y * NZ + z - zq + (zq + e) % 4))
            else:
                send(part_of(first, 0), part_of(first, 0), ysh_s.at[e - 1, i], ysh_r.at[e - 1, i],
                     (s, ((y + e) % NY) * NZ + z))
        relay(n, first)

    def relay_y(i):
        for e in range(1, 4):
            arrived(part_of(y_first(e, i), 0), ysh_s.at[e - 1, i], ysh_r.at[e - 1, i])
            relay(6 + 4 * (e - 1) + i, y_first(e, i))

    def relay_z(i):
        for e in range(1, 4):
            arrived(part_of(z_first(e, i), 0), zsh_s.at[e - 1, i], zsh_r.at[e - 1, i])
            relay(18 + 2 * (e - 1) + i, z_first(e, i))

    def partner_ready():
        for n, (along_z, i) in enumerate(PULLS):
            first = z_first(0, i) if along_z else y_first(0, i)
            arrived(part_of(first, 1), rel_s.at[n], rel_r.at[n])
        for e in range(1, 4):
            for i in range(4):
                n = 6 + 4 * (e - 1) + i
                arrived(part_of(y_first(e, i), 1), rel_s.at[n], rel_r.at[n])
            for i in range(2):
                n = 18 + 2 * (e - 1) + i
                arrived(part_of(z_first(e, i), 1), rel_s.at[n], rel_r.at[n])

    for e in range(1, 8):
        arrived(idxv.at[(s + 8 - e) % 8], pk_s.at[e - 1], pk_r.at[e - 1])
    total = idxv[0]
    for t in range(1, 8):
        total = total + idxv[t]
    tabv[0:8] = total[0:8]
    tabv[8:16] = jnp.where(total[8:16] > 0, total[8:16] - 1, 32)
    to_sm = pltpu.make_async_copy(tabv, tab_sm, loc_sem.at[9])
    to_sm.start()
    to_sm.wait()

    def picked(ref, who, col, first):
        return jnp.concatenate([ref[tab_sm[col, 8 * who + first + u]] for u in range(4)], axis=1)

    def owner(p):
        other = p // 2
        return 2 * (x + other * (xn - x)) + p % 2

    def hidden_pass(j):
        col = 3 * c + j

        def body(p, h):
            xs = picked(xf, p, col, 0)
            ws = w1[j][pl.ds(4 * p, 4)].reshape(512, 128)
            return h + jnp.dot(xs, ws, preferred_element_type=F32)

        hid[j] = lax.fori_loop(0, 8, body, jnp.zeros((256, 128), F32))

    def act_grads(j, full):
        col = 3 * c + j

        def body(p, a):
            vs = jnp.concatenate([w2[j][4 * p + u] for u in range(4)], axis=1)
            ys = picked(full, owner(p), col, 4)
            return a + lax.dot_general(ys, vs, NT, preferred_element_type=F32)

        return lax.fori_loop(0, 4, body, jnp.zeros((256, 128), F32))

    def act_own(j):
        ag_own[j] = act_grads(j, dyf)

    def act_other(j):
        ag_sent[j] = act_grads(j, dyp).astype(BF16)
        send(ag_sent.at[j], ag_got.at[j], ag_s.at[j], ag_r.at[j], (xp * 2 + c, m))

    def activate(j):
        value, slope = gelu_both(hid[j])
        hid[j] = slope
        actt[j] = value.T.astype(BF16)
        send(actt.at[j], actp.at[j], ac_s.at[j], ac_r.at[j], (xp * 2 + c, m))

    def hidden_grads(j):
        arrived(ag_got.at[j], ag_s.at[j], ag_r.at[j])
        grad = (ag_own[j] + ag_got[j].astype(F32)) * hid[j]
        ghcat[:, j * 128:(j + 1) * 128] = grad.astype(BF16)
        ght[j] = grad.T.astype(BF16)

    def grads_one(j):
        col = 3 * c + j

        def body(q, carry):
            who = (2 * xo + q) % 8
            t1 = jnp.dot(ght[j], picked(xf, who, col, 0), preferred_element_type=F32)
            for u in range(4):
                d1[j][4 * who + u] = t1[:, 128 * u:128 * (u + 1)].astype(BF16)
            return carry

        lax.fori_loop(0, 8, body, 0)
        send(d1[j].at[pl.ds(8 * xo, 8)], r1.at[j], s1_s.at[j], s1_r.at[j], (xp * 2 + c, m))
        for co in range(2):
            send(d1[j].at[pl.ds(8 * xp + 4 * co, 4)], rr1.at[col],
                 s2_s.at[j, 1, co], s2_r.at[1, col], (xp * 2 + co, m))
        send(d1[j].at[pl.ds(8 * x + 4 * o, 4)], rp1.at[j], sp_s.at[j, 0], sp_r.at[j, 0], (x * 2 + o, m))

    def grads_two(j):
        col = 3 * c + j
        arrived(actp.at[j], ac_s.at[j], ac_r.at[j])

        def body(p, carry):
            t2 = jnp.dot(actt[j], picked(dyf, owner(p), col, 4), preferred_element_type=F32)
            t2 = t2 + jnp.dot(actp[j], picked(dyp, owner(p), col, 4), preferred_element_type=F32)
            for u in range(4):
                d2[j][4 * p + u] = t2[:, 128 * u:128 * (u + 1)].astype(BF16)
            return carry

        lax.fori_loop(0, 4, body, 0)
        for co in range(2):
            send(d2[j].at[pl.ds(8 + 4 * co, 4)], rn2.at[col],
                 sn_s.at[j, co], sn_r.at[col], (xn * 2 + co, m))
        send(d2[j].at[pl.ds(4 * o, 4)], rp2.at[j], sp_s.at[j, 1], sp_r.at[j, 1], (x * 2 + o, m))

    def grads_added(j):
        col = 3 * c + j
        arrived(r1.at[j], s1_s.at[j], s1_r.at[j])

        def body(k, carry):
            at = 8 * xn + k
            d1[j][at] = (d1[j][at].astype(F32) + r1[j, k].astype(F32)).astype(BF16)
            return carry

        lax.fori_loop(0, 8, body, 0)
        for co in range(2):
            send(d1[j].at[pl.ds(8 * xn + 4 * co, 4)], rl1.at[col],
                 s2_s.at[j, 0, co], s2_r.at[0, col], (xn * 2 + co, m))

    def finish(j):
        for cc, own in ((c, True), (o, False)):
            col = 3 * cc + j
            arrived(rn2.at[col], sn_s.at[j, 0], sn_r.at[col])
            arrived(rl1.at[col], s2_s.at[j, 0, 0], s2_r.at[0, col])
            arrived(rr1.at[col], s2_s.at[j, 1, 0], s2_r.at[1, col])
            if not own:
                arrived(rp1.at[j], sp_s.at[j, 0], sp_r.at[j, 0])
                arrived(rp2.at[j], sp_s.at[j, 1], sp_r.at[j, 1])

            def body(k, carry):
                mine1 = d1[j][4 * s + k] if own else rp1[j, k]
                mine2 = d2[j][4 * c + k] if own else rp2[j, k]
                t1 = mine1.astype(F32) + rl1[col, k].astype(F32) + rr1[col, k].astype(F32)
                t2 = mine2.astype(F32) + rn2[col, k].astype(F32)
                g1_out[col, k] = t1.T.astype(BF16)
                g2_out[col, k] = t2.astype(BF16)
                return carry

            lax.fori_loop(0, 4, body, 0)
            for at, (part, whole) in enumerate(((g1_out, g1_hbm), (g2_out, g2_hbm))):
                cp = pltpu.make_async_copy(part.at[col], whole.at[col], out_sem.at[at, col])
                cp.start()
                leaving.append(cp)

    def group(ref, d, g):
        return ref.at[d, pl.ds(2 * g, 2)]

    def input_group(g):
        for d in D_ORDER:
            yy = (y + d) % NY
            rows = []
            for q in (2 * g, 2 * g + 1):
                base = (yy * NZ + (z + q + 1) % NZ) * 3
                for t in range(3):
                    rows.append(
                        jnp.concatenate(
                            [w1[j][tab_sm[8 + 3 * c + j, base + t]] for j in range(COLS)], axis=1))
            rhs = jnp.concatenate(rows, axis=0)
            out = lax.dot_general(ghcat[...], rhs, NT, preferred_element_type=F32)
            for i in range(2):
                dxo[d, 2 * g + i] = out[:128, 384 * i:384 * (i + 1)]
                pxs[d, 2 * g + i] = out[128:, 384 * i:384 * (i + 1)].astype(BF16)
            send(group(pxs, d, g), group(prx, d, g), px_s.at[d, g], px_r.at[d, g], (x * 2 + o, m))

    def to_y(d, g):
        send(group(prx, d, g), yrc.at[d // 2, pl.ds(2 * g, 2)],
             y_s.at[d // 2, g], y_r.at[d // 2, g], (s, ((y + d) % NY) * NZ + z))

    def input_pair(g):
        step = 1 if g % 2 == 0 else 3
        for d in D_ORDER:
            arrived(group(prx, d, g), px_s.at[d, g], px_r.at[d, g])
            sent = d in (2, 4 - step)

            def body(q, carry):
                both = dxo[d, q] + prx[d, q].astype(F32)
                if sent:
                    prx[d, q] = both.astype(BF16)
                else:
                    dxo[d, q] = both
                return carry

            lax.fori_loop(2 * g, 2 * g + 2, body, 0)
            if d == 2:
                send(group(prx, 2, g), y1b.at[g], y1_s.at[g], y1_r.at[g],
                     (s, ((y + step) % NY) * NZ + z))
            elif sent:
                to_y(d, g)

    def input_added(g):
        d = 1 if g % 2 == 0 else 3
        arrived(y1b.at[g], y1_s.at[g], y1_r.at[g])
        for i in range(2):
            q = 2 * g + i
            prx[d, q] = (dxo[d, q] + y1b[g, i].astype(F32)).astype(BF16)
        to_y(d, g)

    def input_sum(g):
        for i in range(2):
            arrived(yrc.at[i, pl.ds(2 * g, 2)], y_s.at[i, g], y_r.at[i, g])
        for q in (2 * g, 2 * g + 1):
            both = dxo[0, q] + yrc[0, q].astype(F32) + yrc[1, q].astype(F32)
            if q < NZ - 1:
                zs[q] = both.astype(BF16)
                send(zs.at[q], zrc.at[q], z_s.at[q], z_r.at[q], at_z(q + 1))
            else:
                zown[...] = both

    def input_last():
        whole = zown[...]
        for q in range(NZ - 1):
            arrived(zrc.at[q], z_s.at[q], z_r.at[q])
            whole = whole + zrc[q].astype(F32)
        dx_out[...] = whole.astype(BF16)

    pl.semaphore_wait(hello.at[1], 2)
    share(0)
    next_pull()
    share(1)
    next_pull()
    share(2)
    next_pull()
    direct_two(0)
    share(3)
    direct_two(1)
    direct_one(0, xp, way_p)
    share(4)
    direct_two(2)
    direct_one(1, xp, way_p)
    share(5)
    direct_one(2, xp, way_p)
    forward(0, xn, xp, way_p)
    forward(1, xn, xp, way_p)
    forward(2, xn, xp, way_p)
    to_core(0, xf)
    relay_z(0)
    relay_y(0)
    forward(0, xp, xn, way_n)
    arrived(dyf.at[pl.ds(0, 96), pl.ds(128, 128)], xs_s.at[1], xs_r.at[1])
    arrived(xf.at[pl.ds(0, 96), pl.ds(128, 128)], xs_s.at[0], xs_r.at[0])
    relay_z(1)
    relay_y(1)
    forward(1, xp, xn, way_n)
    relay_y(2)
    complete_two(0)
    act_own(0)
    relay_y(3)
    forward(2, xp, xn, way_n)
    complete_two(1)
    complete_two(2)
    partner_ready()
    act_other(0)
    act_other(1)
    act_other(2)
    act_own(1)
    act_own(2)
    complete_one(0)
    hidden_pass(0)
    activate(0)
    hidden_grads(0)
    complete_one(1)
    hidden_pass(1)
    activate(1)
    hidden_grads(1)
    grads_one(0)
    complete_one(2)
    hidden_pass(2)
    activate(2)
    hidden_grads(2)
    input_group(0)
    grads_two(0)
    input_group(1)
    input_pair(0)
    grads_added(0)
    grads_one(1)
    input_group(2)
    input_pair(1)
    input_added(0)
    grads_two(1)
    grads_one(2)
    input_group(3)
    input_pair(2)
    input_added(1)
    grads_added(1)
    grads_two(2)
    input_sum(0)
    input_pair(3)
    input_added(2)
    input_sum(1)
    input_added(3)
    grads_added(2)
    input_sum(2)
    finish(0)
    input_sum(3)
    finish(1)
    input_last()
    finish(2)
    for cp in pending + pulls[-2:]:
        cp.wait_send()
    for cp in leaving:
        cp.wait()


def copy_out(dx, g1, g2, dx_out, g1_out, g2_out, dx_v, g1_v, g2_v, sem):
    steps = [(dx, dx_v, dx_out)]
    for col in range(6):
        steps.append((g1.at[col], g1_v.at[col], g1_out.at[col]))
        steps.append((g2.at[col], g2_v.at[col], g2_out.at[col]))
    reads = [pltpu.make_async_copy(a, v, sem.at[0, n]) for n, (a, v, b) in enumerate(steps)]
    writes = [pltpu.make_async_copy(v, b, sem.at[1, n]) for n, (a, v, b) in enumerate(steps)]
    for cp in reads:
        cp.start()
    for read, write in zip(reads, writes):
        read.wait()
        write.start()
    for cp in writes:
        cp.wait()


def per_device(inputs, out_grads, w1_blocks, w1_rows, w1_count, w2_blocks, w2_cols, w2_count):
    any_space = pl.BlockSpec(memory_space=pl.ANY)
    vmem = pl.BlockSpec(memory_space=pltpu.VMEM)
    smem = pl.BlockSpec(memory_space=pltpu.SMEM)
    dma = pltpu.SemaphoreType.DMA
    w_scratch = [pltpu.VMEM((33, 128, 128), BF16)] * 3 + [pltpu.VMEM((16, 128, 128), BF16)] * 3
    d_scratch = [pltpu.VMEM((32, 128, 128), BF16)] * 3 + [pltpu.VMEM((16, 128, 128), BF16)] * 3
    shapes = (
        jax.ShapeDtypeStruct((128, 384), BF16),
        jax.ShapeDtypeStruct((6, 4, 128, 128), BF16),
        jax.ShapeDtypeStruct((6, 4, 128, 128), BF16),
    )
    grads = pl.pallas_call(
        kernel,
        out_shape=shapes,
        in_specs=[any_space] * 4 + [smem] * 4,
        out_specs=(vmem, any_space, any_space),
        scratch_shapes=[
            pltpu.VMEM((128, 12288), BF16),
            pltpu.VMEM((128, 12288), BF16),
            pltpu.VMEM((97, 256, 128), BF16),
            pltpu.VMEM((97, 256, 128), BF16),
            pltpu.VMEM((97, 256, 128), BF16),
            *w_scratch,
            pltpu.VMEM((16, 128), jnp.int32),
            pltpu.VMEM((8, 16, 128), jnp.int32),
            pltpu.VMEM((16, 128), jnp.int32),
            pltpu.SMEM((16, 128), jnp.int32),
            *[pltpu.VMEM((3, 256, 128), F32)] * 2,
            *[pltpu.VMEM((3, 256, 128), BF16)] * 2,
            pltpu.VMEM((256, 384), BF16),
            *[pltpu.VMEM((3, 128, 256), BF16)] * 3,
            *d_scratch,
            pltpu.VMEM((3, 8, 128, 128), BF16),
            pltpu.VMEM((6, 4, 128, 128), BF16),
            pltpu.VMEM((6, 4, 128, 128), BF16),
            pltpu.VMEM((6, 4, 128, 128), BF16),
            pltpu.VMEM((3, 4, 128, 128), BF16),
            pltpu.VMEM((3, 4, 128, 128), BF16),
            pltpu.VMEM((6, 4, 128, 128), BF16),
            pltpu.VMEM((6, 4, 128, 128), BF16),
            pltpu.VMEM((4, 8, 128, 384), F32),
            pltpu.VMEM((4, 8, 128, 384), BF16),
            pltpu.VMEM((4, 8, 128, 384), BF16),
            pltpu.VMEM((4, 2, 128, 384), BF16),
            pltpu.VMEM((2, 8, 128, 384), BF16),
            pltpu.VMEM((7, 128, 384), BF16),
            pltpu.VMEM((128, 384), F32),
            pltpu.VMEM((7, 128, 384), BF16),
            dma((2, 6)),
            pltpu.SemaphoreType.REGULAR((2,)),
            dma((11,)),
            dma((7,)), dma((7,)),
            dma((2,)), dma((2,)),
            dma((3, 2, 2)), dma((3, 2, 2)),
            dma((3, 2)), dma((3, 2)),
            dma((3, 2)), dma((3, 2)),
            dma((3, 2)), dma((3, 2)),
            dma((6,)), dma((6,)),
            dma((3, 4)), dma((3, 4)),
            dma((3, 2)), dma((3, 2)),
            dma((24,)), dma((24,)),
            dma((3,)), dma((3,)),
            dma((3,)), dma((3,)),
            dma((3,)), dma((3,)),
            dma((3, 2, 2)), dma((2, 6)),
            dma((3, 2)), dma((6,)),
            dma((3, 2)), dma((3, 2)),
            dma((4, 4)), dma((4, 4)),
            dma((4,)), dma((4,)),
            dma((2, 4)), dma((2, 4)),
            dma((7,)), dma((7,)),
        ],
        compiler_params=pltpu.CompilerParams(
            collective_id=0, has_side_effects=True, vmem_limit_bytes=60 * 1024 * 1024),
    )(inputs, out_grads, w1_blocks, w2_blocks, w1_rows.T, w1_count, w2_cols.T, w2_count)
    return pl.pallas_call(
        copy_out,
        out_shape=shapes,
        in_specs=[any_space] * 3,
        out_specs=(any_space,) * 3,
        scratch_shapes=[
            pltpu.VMEM((128, 384), BF16),
            pltpu.VMEM((6, 4, 128, 128), BF16),
            pltpu.VMEM((6, 4, 128, 128), BF16),
            dma((2, 13)),
        ],
    )(*grads)


def solution(mesh):
    in_specs = (
        P("seq", None),
        P("seq", None),
        P("mp", "seq", None, None),
        P("mp", "seq"),
        P("mp"),
        P("mp", "seq", None, None),
        P("mp", "seq"),
        P("mp"),
    )
    out_specs = (P("seq", "mp"), P("mp", "seq", None, None), P("mp", "seq", None, None))
    return jax.shard_map(
        per_device, mesh=mesh, in_specs=in_specs, out_specs=out_specs, check_vma=False
    )
```

```python
import jax
import jax.numpy as jnp
from jax import lax
from jax.experimental import pallas as pl
from jax.experimental.pallas import tpu as pltpu
from jax.sharding import PartitionSpec as P

GELU_C = 0.7978845608028654
CUBIC = 0.044715
BF16 = jnp.bfloat16
F32 = jnp.float32
MESH = pl.DeviceIdType.MESH
NT = (((1,), (1,)), ((), ()))

NX = 4
NY = 4
NZ = 8
COLS = 3
D_ORDER = (2, 1, 3, 0)
PULLS = ((True, 0), (False, 0), (True, 1), (False, 1), (False, 2), (False, 3))


def gelu_both(h):
    arg = GELU_C * (h + CUBIC * h * h * h)
    t = jnp.tanh(arg)
    value = 0.5 * h * (1.0 + t)
    slope = 0.5 * (1.0 + t) + 0.5 * h * (1.0 - t * t) * GELU_C * (1.0 + 3.0 * CUBIC * h * h)
    return value, slope


def kernel(
    x_hbm, dy_hbm, w1_hbm, w2_hbm, rows_sm, count1_sm, cols_sm, count2_sm,
    dx_out, g1_hbm, g2_hbm,
    stx, sty, xf, dyf, dyp, w1a, w1b, w1c, w2a, w2b, w2c,
    pktv, idxv, tabv, tab_sm,
    hid, ag_own, ag_sent, ag_got, ghcat, ght, actt, actp,
    d1a, d1b, d1c, d2a, d2b, d2c,
    r1, rl1, rr1, rn2, rp1, rp2,
    g1_out, g2_out, dxo, pxs, prx, y1b, yrc, zs, zown, zrc,
    out_sem, hello, loc_sem, pk_s, pk_r, xs_s, xs_r, wd_s, wd_r, wn_s, wn_r, wp_s, wp_r, wf_s, wf_r,
    pull_s, pull_r, ysh_s, ysh_r, zsh_s, zsh_r, rel_s, rel_r, ag_s, ag_r, ac_s, ac_r,
    s1_s, s1_r, s2_s, s2_r, sn_s, sn_r, sp_s, sp_r, px_s, px_r, y1_s, y1_r, y_s, y_r, z_s, z_r,
):
    w1 = (w1a, w1b, w1c)
    w2 = (w2a, w2b, w2c)
    d1 = (d1a, d1b, d1c)
    d2 = (d2a, d2b, d2c)
    s = lax.axis_index("seq")
    m = lax.axis_index("mp")
    x = s // 2
    c = s % 2
    o = 1 - c
    xl = (x + 3) % 4
    xr = (x + 1) % 4
    xo = (x + 2) % 4
    xp = x + 1 - 2 * (x % 2)
    xn = 3 - x
    y = m // NZ
    z = m % NZ
    zq = z % 4
    way_p = x % 2
    way_n = 1 - way_p
    pending = []
    leaving = []

    def send(src, dst, ssem, rsem, dev):
        cp = pltpu.make_async_remote_copy(
            src_ref=src, dst_ref=dst, send_sem=ssem, recv_sem=rsem,
            device_id=dev, device_id_type=MESH,
        )
        cp.start()
        pending.append(cp)

    def arrived(ref, ssem, rsem):
        pltpu.make_async_remote_copy(
            src_ref=ref, dst_ref=ref, send_sem=ssem, recv_sem=rsem,
            device_id=(s, m), device_id_type=MESH,
        ).wait_recv()

    local = [
        pltpu.make_async_copy(x_hbm, stx, loc_sem.at[0]),
        pltpu.make_async_copy(dy_hbm, sty, loc_sem.at[1]),
    ]
    wlocal = []
    for j in range(COLS):
        wlocal.append(
            (
                pltpu.make_async_copy(
                    w1_hbm.at[3 * c + j], w1[j].at[pl.ds(4 * s, 4)], loc_sem.at[3 + 2 * j]),
                pltpu.make_async_copy(
                    w2_hbm.at[3 * c + j], w2[j].at[pl.ds(4 * c, 4)], loc_sem.at[4 + 2 * j]),
            )
        )
    for cp in local:
        cp.start()
    for pair in wlocal:
        for cp in pair:
            cp.start()

    def at_z(e):
        return (s, y * NZ + (z + e) % NZ)

    barrier = pltpu.get_barrier_semaphore()
    for e in range(1, 8):
        pl.semaphore_signal(barrier, inc=1, device_id=((s + e) % 8, m), device_id_type=MESH)
    for e in range(1, NY):
        pl.semaphore_signal(
            barrier, inc=1, device_id=(s, ((y + e) % NY) * NZ + z), device_id_type=MESH)
    for e in (1, NZ - 1):
        pl.semaphore_signal(barrier, inc=1, device_id=at_z(e), device_id_type=MESH)

    sub = lax.broadcasted_iota(jnp.int32, (8, 128), 0)
    lane = lax.broadcasted_iota(jnp.int32, (8, 128), 1)
    named = jnp.zeros((8, 128), jnp.int32)
    slot_of = jnp.zeros((8, 128), jnp.int32)
    for col in range(6):
        for k in range(4):
            slot = 4 * s + k
            row = jnp.where(slot < count1_sm[col], rows_sm[k, col], 96)
            other = jnp.where(slot < count2_sm[col], cols_sm[k, col], 96)
            named = jnp.where((sub == col) & (lane == 8 * s + k), row, named)
            named = jnp.where((sub == col) & (lane == 8 * s + 4 + k), other, named)
            slot_of = jnp.where((sub == col) & (lane == row), slot + 1, slot_of)
    pktv[0:8] = named
    pktv[8:16] = slot_of

    def regrouped(at, flat, full):
        local[at].wait()

        def body(r, carry):
            full[r, 0:128] = flat[:, pl.ds(pl.multiple_of(r * 128, 128), 128)]
            return carry

        lax.fori_loop(0, 96, body, 0, unroll=8)
        full[96] = jnp.zeros((256, 128), BF16)

    pl.semaphore_wait(barrier, 7 + NY - 1 + 2)

    pulls = []

    def pull():
        n = len(pulls)
        along_z, i = PULLS[n]
        first = 64 + 8 * zq + 4 * i if along_z else 16 * y + 4 * i
        send(dyf.at[pl.ds(first, 4), pl.ds(0, 128)], dyp.at[pl.ds(first, 4), pl.ds(0, 128)],
             pull_s.at[n], pull_r.at[n], (xp * 2 + c, m))
        pulls.append(pending.pop())

    def next_pull():
        pulls[len(pulls) - 2].wait_send()
        pull()

    for e in range(1, 8):
        send(pktv, idxv.at[s], pk_s.at[e - 1], pk_r.at[e - 1], ((s + e) % 8, m))
    idxv[s] = pktv[...]
    for e in (1, NZ - 1):
        pl.semaphore_signal(hello.at[0], inc=1, device_id=at_z(e), device_id_type=MESH)

    def direct_one(j, xd, way):
        for cd in range(2):
            send(w1_hbm.at[3 * cd + j], w1[j].at[pl.ds(4 * s, 4)],
                 wd_s.at[j, way, cd], wd_r.at[j, way, c], (xd * 2 + cd, m))

    def core_one(j):
        send(w1_hbm.at[3 * o + j], w1[j].at[pl.ds(4 * s, 4)],
             wp_s.at[j, 0], wp_r.at[j, 0], (x * 2 + o, m))

    def direct_two(j):
        for cd in range(2):
            send(w2_hbm.at[3 * cd + j], w2[j].at[pl.ds(8 + 4 * c, 4)],
                 wn_s.at[j, cd], wn_r.at[j, c], (xn * 2 + cd, m))
        send(w2_hbm.at[3 * o + j], w2[j].at[pl.ds(4 * c, 4)],
             wp_s.at[j, 1], wp_r.at[j, 1], (x * 2 + o, m))

    def from_chip(j, xs, way, cs):
        arrived(w1[j].at[pl.ds(8 * xs + 4 * cs, 4)], wd_s.at[j, way, cs], wd_r.at[j, way, cs])

    def forward(j, xs, xd, way):
        from_chip(j, xs, way, way)
        part = w1[j].at[pl.ds(8 * xs + 4 * way, 4)]
        send(part, part, wf_s.at[j, way], wf_r.at[j, way], (xd * 2 + c, m))

    def complete_one(j):
        wlocal[j][0].wait()
        arrived(w1[j].at[pl.ds(8 * x + 4 * o, 4)], wp_s.at[j, 0], wp_r.at[j, 0])
        from_chip(j, xn, way_p, 1 - way_p)
        from_chip(j, xp, way_n, 1 - way_n)
        for way in range(2):
            arrived(w1[j].at[pl.ds(8 * xo + 4 * way, 4)], wf_s.at[j, way], wf_r.at[j, way])

    def complete_two(j):
        wlocal[j][1].wait()
        arrived(w2[j].at[pl.ds(4 * o, 4)], wp_s.at[j, 1], wp_r.at[j, 1])
        for cs in range(2):
            arrived(w2[j].at[pl.ds(8 + 4 * cs, 4)], wn_s.at[j, cs], wn_r.at[j, cs])

    for j in range(COLS):
        direct_one(j, xn, way_n)

    def to_core(at, full):
        send(full.at[pl.ds(0, 96), pl.ds(0, 128)], full.at[pl.ds(0, 96), pl.ds(128, 128)],
             xs_s.at[at], xs_r.at[at], (x * 2 + o, m))

    regrouped(1, sty, dyf)
    pull()
    pull()
    for j in range(COLS):
        core_one(j)
    regrouped(0, stx, xf)
    to_core(1, dyf)
    next_pull()
    dyp[96] = jnp.zeros((256, 128), BF16)

    for j in range(COLS):
        w1[j][32] = jnp.zeros((128, 128), BF16)

    pl.semaphore_wait(hello.at[0], 2)
    for e in (2, NZ - 2):
        pl.semaphore_signal(hello.at[1], inc=1, device_id=at_z(e), device_id_type=MESH)

    def part_of(first, half):
        return dyp.at[pl.ds(first, 4), pl.ds(128 * half, 128)]

    def relay(n, first):
        send(part_of(first, 0), part_of(first, 1), rel_s.at[n], rel_r.at[n], (x * 2 + o, m))

    def y_first(e, i):
        return 16 * ((y + 4 - e) % 4) + 4 * i

    def z_first(e, i):
        return 64 + 8 * ((zq + 4 - e) % 4) + 4 * i

    def share(n):
        along_z, i = PULLS[n]
        first = z_first(0, i) if along_z else y_first(0, i)
        arrived(part_of(first, 0), pull_s.at[n], pull_r.at[n])
        for e in (1, 3, 2):
            if along_z:
                send(part_of(first, 0), part_of(first, 0), zsh_s.at[e - 1, i], zsh_r.at[e - 1, i],
                     (s, y * NZ + z - zq + (zq + e) % 4))
            else:
                send(part_of(first, 0), part_of(first, 0), ysh_s.at[e - 1, i], ysh_r.at[e - 1, i],
                     (s, ((y + e) % NY) * NZ + z))
        relay(n, first)

    def relay_y(i):
        for e in range(1, 4):
            arrived(part_of(y_first(e, i), 0), ysh_s.at[e - 1, i], ysh_r.at[e - 1, i])
            relay(6 + 4 * (e - 1) + i, y_first(e, i))

    def relay_z(i):
        for e in range(1, 4):
            arrived(part_of(z_first(e, i), 0), zsh_s.at[e - 1, i], zsh_r.at[e - 1, i])
            relay(18 + 2 * (e - 1) + i, z_first(e, i))

    def partner_ready():
        for n, (along_z, i) in enumerate(PULLS):
            first = z_first(0, i) if along_z else y_first(0, i)
            arrived(part_of(first, 1), rel_s.at[n], rel_r.at[n])
        for e in range(1, 4):
            for i in range(4):
                n = 6 + 4 * (e - 1) + i
                arrived(part_of(y_first(e, i), 1), rel_s.at[n], rel_r.at[n])
            for i in range(2):
                n = 18 + 2 * (e - 1) + i
                arrived(part_of(z_first(e, i), 1), rel_s.at[n], rel_r.at[n])

    for e in range(1, 8):
        arrived(idxv.at[(s + 8 - e) % 8], pk_s.at[e - 1], pk_r.at[e - 1])
    total = idxv[0]
    for t in range(1, 8):
        total = total + idxv[t]
    tabv[0:8] = total[0:8]
    tabv[8:16] = jnp.where(total[8:16] > 0, total[8:16] - 1, 32)
    to_sm = pltpu.make_async_copy(tabv, tab_sm, loc_sem.at[9])
    to_sm.start()
    to_sm.wait()

    def picked(ref, who, col, first):
        return jnp.concatenate([ref[tab_sm[col, 8 * who + first + u]] for u in range(4)], axis=1)

    def owner(p):
        other = p // 2
        return 2 * (x + other * (xn - x)) + p % 2

    def hidden_pass(j):
        col = 3 * c + j

        def body(p, h):
            xs = picked(xf, p, col, 0)
            ws = w1[j][pl.ds(4 * p, 4)].reshape(512, 128)
            return h + jnp.dot(xs, ws, preferred_element_type=F32)

        hid[j] = lax.fori_loop(0, 8, body, jnp.zeros((256, 128), F32))

    def act_grads(j, full):
        col = 3 * c + j

        def body(p, a):
            vs = jnp.concatenate([w2[j][4 * p + u] for u in range(4)], axis=1)
            ys = picked(full, owner(p), col, 4)
            return a + lax.dot_general(ys, vs, NT, preferred_element_type=F32)

        return lax.fori_loop(0, 4, body, jnp.zeros((256, 128), F32))

    def act_own(j):
        ag_own[j] = act_grads(j, dyf)

    def act_other(j):
        ag_sent[j] = act_grads(j, dyp).astype(BF16)
        send(ag_sent.at[j], ag_got.at[j], ag_s.at[j], ag_r.at[j], (xp * 2 + c, m))

    def activate(j):
        value, slope = gelu_both(hid[j])
        hid[j] = slope
        actt[j] = value.T.astype(BF16)
        send(actt.at[j], actp.at[j], ac_s.at[j], ac_r.at[j], (xp * 2 + c, m))

    def hidden_grads(j):
        arrived(ag_got.at[j], ag_s.at[j], ag_r.at[j])
        grad = (ag_own[j] + ag_got[j].astype(F32)) * hid[j]
        ghcat[:, j * 128:(j + 1) * 128] = grad.astype(BF16)
        ght[j] = grad.T.astype(BF16)

    def grads_one(j):
        col = 3 * c + j

        def body(q, carry):
            who = (2 * xo + q) % 8
            t1 = jnp.dot(ght[j], picked(xf, who, col, 0), preferred_element_type=F32)
            for u in range(4):
                d1[j][4 * who + u] = t1[:, 128 * u:128 * (u + 1)].astype(BF16)
            return carry

        lax.fori_loop(0, 8, body, 0)
        send(d1[j].at[pl.ds(8 * xo, 8)], r1.at[j], s1_s.at[j], s1_r.at[j], (xp * 2 + c, m))
        for co in range(2):
            send(d1[j].at[pl.ds(8 * xp + 4 * co, 4)], rr1.at[col],
                 s2_s.at[j, 1, co], s2_r.at[1, col], (xp * 2 + co, m))
        send(d1[j].at[pl.ds(8 * x + 4 * o, 4)], rp1.at[j], sp_s.at[j, 0], sp_r.at[j, 0], (x * 2 + o, m))

    def grads_two(j):
        col = 3 * c + j
        arrived(actp.at[j], ac_s.at[j], ac_r.at[j])

        def body(p, carry):
            t2 = jnp.dot(actt[j], picked(dyf, owner(p), col, 4), preferred_element_type=F32)
            t2 = t2 + jnp.dot(actp[j], picked(dyp, owner(p), col, 4), preferred_element_type=F32)
            for u in range(4):
                d2[j][4 * p + u] = t2[:, 128 * u:128 * (u + 1)].astype(BF16)
            return carry

        lax.fori_loop(0, 4, body, 0)
        for co in range(2):
            send(d2[j].at[pl.ds(8 + 4 * co, 4)], rn2.at[col],
                 sn_s.at[j, co], sn_r.at[col], (xn * 2 + co, m))
        send(d2[j].at[pl.ds(4 * o, 4)], rp2.at[j], sp_s.at[j, 1], sp_r.at[j, 1], (x * 2 + o, m))

    def grads_added(j):
        col = 3 * c + j
        arrived(r1.at[j], s1_s.at[j], s1_r.at[j])

        def body(k, carry):
            at = 8 * xn + k
            d1[j][at] = (d1[j][at].astype(F32) + r1[j, k].astype(F32)).astype(BF16)
            return carry

        lax.fori_loop(0, 8, body, 0)
        for co in range(2):
            send(d1[j].at[pl.ds(8 * xn + 4 * co, 4)], rl1.at[col],
                 s2_s.at[j, 0, co], s2_r.at[0, col], (xn * 2 + co, m))

    def finish(j):
        for cc, own in ((c, True), (o, False)):
            col = 3 * cc + j
            arrived(rn2.at[col], sn_s.at[j, 0], sn_r.at[col])
            arrived(rl1.at[col], s2_s.at[j, 0, 0], s2_r.at[0, col])
            arrived(rr1.at[col], s2_s.at[j, 1, 0], s2_r.at[1, col])
            if not own:
                arrived(rp1.at[j], sp_s.at[j, 0], sp_r.at[j, 0])
                arrived(rp2.at[j], sp_s.at[j, 1], sp_r.at[j, 1])

            def body(k, carry):
                mine1 = d1[j][4 * s + k] if own else rp1[j, k]
                mine2 = d2[j][4 * c + k] if own else rp2[j, k]
                t1 = mine1.astype(F32) + rl1[col, k].astype(F32) + rr1[col, k].astype(F32)
                t2 = mine2.astype(F32) + rn2[col, k].astype(F32)
                g1_out[col, k] = t1.T.astype(BF16)
                g2_out[col, k] = t2.astype(BF16)
                return carry

            lax.fori_loop(0, 4, body, 0)
            for at, (part, whole) in enumerate(((g1_out, g1_hbm), (g2_out, g2_hbm))):
                cp = pltpu.make_async_copy(part.at[col], whole.at[col], out_sem.at[at, col])
                cp.start()
                leaving.append(cp)

    def group(ref, d, g):
        return ref.at[d, pl.ds(2 * g, 2)]

    def input_group(g):
        for d in D_ORDER:
            yy = (y + d) % NY
            rows = []
            for q in (2 * g, 2 * g + 1):
                base = (yy * NZ + (z + q + 1) % NZ) * 3
                for t in range(3):
                    rows.append(
                        jnp.concatenate(
                            [w1[j][tab_sm[8 + 3 * c + j, base + t]] for j in range(COLS)], axis=1))
            rhs = jnp.concatenate(rows, axis=0)
            out = lax.dot_general(ghcat[...], rhs, NT, preferred_element_type=F32)
            for i in range(2):
                dxo[d, 2 * g + i] = out[:128, 384 * i:384 * (i + 1)]
                pxs[d, 2 * g + i] = out[128:, 384 * i:384 * (i + 1)].astype(BF16)
            send(group(pxs, d, g), group(prx, d, g), px_s.at[d, g], px_r.at[d, g], (x * 2 + o, m))

    def to_y(d, g):
        send(group(prx, d, g), yrc.at[d // 2, pl.ds(2 * g, 2)],
             y_s.at[d // 2, g], y_r.at[d // 2, g], (s, ((y + d) % NY) * NZ + z))

    def input_pair(g):
        step = 1 if g % 2 == 0 else 3
        for d in D_ORDER:
            arrived(group(prx, d, g), px_s.at[d, g], px_r.at[d, g])
            sent = d in (2, 4 - step)

            def body(q, carry):
                both = dxo[d, q] + prx[d, q].astype(F32)
                if sent:
                    prx[d, q] = both.astype(BF16)
                else:
                    dxo[d, q] = both
                return carry

            lax.fori_loop(2 * g, 2 * g + 2, body, 0)
            if d == 2:
                send(group(prx, 2, g), y1b.at[g], y1_s.at[g], y1_r.at[g],
                     (s, ((y + step) % NY) * NZ + z))
            elif sent:
                to_y(d, g)

    def input_added(g):
        d = 1 if g % 2 == 0 else 3
        arrived(y1b.at[g], y1_s.at[g], y1_r.at[g])
        for i in range(2):
            q = 2 * g + i
            prx[d, q] = (dxo[d, q] + y1b[g, i].astype(F32)).astype(BF16)
        to_y(d, g)

    def input_sum(g):
        for i in range(2):
            arrived(yrc.at[i, pl.ds(2 * g, 2)], y_s.at[i, g], y_r.at[i, g])
        for q in (2 * g, 2 * g + 1):
            both = dxo[0, q] + yrc[0, q].astype(F32) + yrc[1, q].astype(F32)
            if q < NZ - 1:
                zs[q] = both.astype(BF16)
                send(zs.at[q], zrc.at[q], z_s.at[q], z_r.at[q], at_z(q + 1))
            else:
                zown[...] = both

    def input_last():
        whole = zown[...]
        for q in range(NZ - 1):
            arrived(zrc.at[q], z_s.at[q], z_r.at[q])
            whole = whole + zrc[q].astype(F32)
        dx_out[...] = whole.astype(BF16)

    pl.semaphore_wait(hello.at[1], 2)
    share(0)
    next_pull()
    share(1)
    next_pull()
    share(2)
    next_pull()
    direct_two(0)
    share(3)
    direct_two(1)
    direct_one(0, xp, way_p)
    share(4)
    direct_two(2)
    direct_one(1, xp, way_p)
    share(5)
    direct_one(2, xp, way_p)
    forward(0, xn, xp, way_p)
    forward(1, xn, xp, way_p)
    forward(2, xn, xp, way_p)
    to_core(0, xf)
    relay_z(0)
    relay_y(0)
    forward(0, xp, xn, way_n)
    arrived(dyf.at[pl.ds(0, 96), pl.ds(128, 128)], xs_s.at[1], xs_r.at[1])
    arrived(xf.at[pl.ds(0, 96), pl.ds(128, 128)], xs_s.at[0], xs_r.at[0])
    relay_z(1)
    relay_y(1)
    forward(1, xp, xn, way_n)
    relay_y(2)
    complete_two(0)
    act_own(0)
    relay_y(3)
    forward(2, xp, xn, way_n)
    complete_two(1)
    act_own(1)
    complete_two(2)
    act_own(2)
    partner_ready()
    act_other(0)
    act_other(1)
    act_other(2)
    complete_one(0)
    hidden_pass(0)
    activate(0)
    hidden_grads(0)
    complete_one(1)
    hidden_pass(1)
    activate(1)
    hidden_grads(1)
    grads_one(0)
    complete_one(2)
    hidden_pass(2)
    activate(2)
    hidden_grads(2)
    input_group(0)
    grads_two(0)
    input_group(1)
    input_pair(0)
    grads_added(0)
    grads_one(1)
    input_group(2)
    input_pair(1)
    input_added(0)
    grads_two(1)
    grads_one(2)
    input_group(3)
    input_pair(2)
    input_added(1)
    grads_added(1)
    grads_two(2)
    input_sum(0)
    input_pair(3)
    input_added(2)
    input_sum(1)
    input_added(3)
    grads_added(2)
    input_sum(2)
    finish(0)
    input_sum(3)
    finish(1)
    input_last()
    finish(2)
    for cp in pending + pulls[-2:]:
        cp.wait_send()
    for cp in leaving:
        cp.wait()


def copy_out(dx, g1, g2, dx_out, g1_out, g2_out, dx_v, g1_v, g2_v, sem):
    steps = [(dx, dx_v, dx_out)]
    for col in range(6):
        steps.append((g1.at[col], g1_v.at[col], g1_out.at[col]))
        steps.append((g2.at[col], g2_v.at[col], g2_out.at[col]))
    reads = [pltpu.make_async_copy(a, v, sem.at[0, n]) for n, (a, v, b) in enumerate(steps)]
    writes = [pltpu.make_async_copy(v, b, sem.at[1, n]) for n, (a, v, b) in enumerate(steps)]
    for cp in reads:
        cp.start()
    for read, write in zip(reads, writes):
        read.wait()
        write.start()
    for cp in writes:
        cp.wait()


def per_device(inputs, out_grads, w1_blocks, w1_rows, w1_count, w2_blocks, w2_cols, w2_count):
    any_space = pl.BlockSpec(memory_space=pl.ANY)
    vmem = pl.BlockSpec(memory_space=pltpu.VMEM)
    smem = pl.BlockSpec(memory_space=pltpu.SMEM)
    dma = pltpu.SemaphoreType.DMA
    w_scratch = [pltpu.VMEM((33, 128, 128), BF16)] * 3 + [pltpu.VMEM((16, 128, 128), BF16)] * 3
    d_scratch = [pltpu.VMEM((32, 128, 128), BF16)] * 3 + [pltpu.VMEM((16, 128, 128), BF16)] * 3
    shapes = (
        jax.ShapeDtypeStruct((128, 384), BF16),
        jax.ShapeDtypeStruct((6, 4, 128, 128), BF16),
        jax.ShapeDtypeStruct((6, 4, 128, 128), BF16),
    )
    grads = pl.pallas_call(
        kernel,
        out_shape=shapes,
        in_specs=[any_space] * 4 + [smem] * 4,
        out_specs=(vmem, any_space, any_space),
        scratch_shapes=[
            pltpu.VMEM((128, 12288), BF16),
            pltpu.VMEM((128, 12288), BF16),
            pltpu.VMEM((97, 256, 128), BF16),
            pltpu.VMEM((97, 256, 128), BF16),
            pltpu.VMEM((97, 256, 128), BF16),
            *w_scratch,
            pltpu.VMEM((16, 128), jnp.int32),
            pltpu.VMEM((8, 16, 128), jnp.int32),
            pltpu.VMEM((16, 128), jnp.int32),
            pltpu.SMEM((16, 128), jnp.int32),
            *[pltpu.VMEM((3, 256, 128), F32)] * 2,
            *[pltpu.VMEM((3, 256, 128), BF16)] * 2,
            pltpu.VMEM((256, 384), BF16),
            *[pltpu.VMEM((3, 128, 256), BF16)] * 3,
            *d_scratch,
            pltpu.VMEM((3, 8, 128, 128), BF16),
            pltpu.VMEM((6, 4, 128, 128), BF16),
            pltpu.VMEM((6, 4, 128, 128), BF16),
            pltpu.VMEM((6, 4, 128, 128), BF16),
            pltpu.VMEM((3, 4, 128, 128), BF16),
            pltpu.VMEM((3, 4, 128, 128), BF16),
            pltpu.VMEM((6, 4, 128, 128), BF16),
            pltpu.VMEM((6, 4, 128, 128), BF16),
            pltpu.VMEM((4, 8, 128, 384), F32),
            pltpu.VMEM((4, 8, 128, 384), BF16),
            pltpu.VMEM((4, 8, 128, 384), BF16),
            pltpu.VMEM((4, 2, 128, 384), BF16),
            pltpu.VMEM((2, 8, 128, 384), BF16),
            pltpu.VMEM((7, 128, 384), BF16),
            pltpu.VMEM((128, 384), F32),
            pltpu.VMEM((7, 128, 384), BF16),
            dma((2, 6)),
            pltpu.SemaphoreType.REGULAR((2,)),
            dma((11,)),
            dma((7,)), dma((7,)),
            dma((2,)), dma((2,)),
            dma((3, 2, 2)), dma((3, 2, 2)),
            dma((3, 2)), dma((3, 2)),
            dma((3, 2)), dma((3, 2)),
            dma((3, 2)), dma((3, 2)),
            dma((6,)), dma((6,)),
            dma((3, 4)), dma((3, 4)),
            dma((3, 2)), dma((3, 2)),
            dma((24,)), dma((24,)),
            dma((3,)), dma((3,)),
            dma((3,)), dma((3,)),
            dma((3,)), dma((3,)),
            dma((3, 2, 2)), dma((2, 6)),
            dma((3, 2)), dma((6,)),
            dma((3, 2)), dma((3, 2)),
            dma((4, 4)), dma((4, 4)),
            dma((4,)), dma((4,)),
            dma((2, 4)), dma((2, 4)),
            dma((7,)), dma((7,)),
        ],
        compiler_params=pltpu.CompilerParams(
            collective_id=0, has_side_effects=True, vmem_limit_bytes=60 * 1024 * 1024),
    )(inputs, out_grads, w1_blocks, w2_blocks, w1_rows.T, w1_count, w2_cols.T, w2_count)
    return pl.pallas_call(
        copy_out,
        out_shape=shapes,
        in_specs=[any_space] * 3,
        out_specs=(any_space,) * 3,
        scratch_shapes=[
            pltpu.VMEM((128, 384), BF16),
            pltpu.VMEM((6, 4, 128, 128), BF16),
            pltpu.VMEM((6, 4, 128, 128), BF16),
            dma((2, 13)),
        ],
    )(*grads)


def solution(mesh):
    in_specs = (
        P("seq", None),
        P("seq", None),
        P("mp", "seq", None, None),
        P("mp", "seq"),
        P("mp"),
        P("mp", "seq", None, None),
        P("mp", "seq"),
        P("mp"),
    )
    out_specs = (P("seq", "mp"), P("mp", "seq", None, None), P("mp", "seq", None, None))
    return jax.shard_map(
        per_device, mesh=mesh, in_specs=in_specs, out_specs=out_specs, check_vma=False
    )
```
